32 devices in a mesh: stream: 8 (over z, x), span: 4 (over y, core).
Axes of the slice: x: 2, y: 2, z: 4, core: 2. Of those that a mesh axis runs over, the one named last changes fastest.
Arguments:
- rhs: float32 [8, 4, 2, 320, 128], P('stream', 'span'), may hold values from -6 to 6
- inv_blocks: bfloat16 [8, 4, 2, 320, 320], P('stream', 'span')
- coupling: bfloat16 [6, 320, 320], replicated, may hold values from -0.109375 to 0.109375
- trace_ops: bfloat16 [4, 80, 320], replicated, may hold values from -0.3125 to 0.3125
- lift_ops: bfloat16 [4, 320, 80], replicated
- order: int32 [8, 4, 2], P('stream', 'span'), may hold values from 0 to 1, each once within a row
- counts: int32 [8, 4], P('stream', 'span'), may hold values from 1 to 2, as said below
- neighbours: int32 [8, 4, 2, 2], P('stream', 'span'), may hold values from 0 to 2, as said below
- face_ids: int32 [8, 4, 2, 2], P('stream', 'span'), may hold values from 0 to 5
Outputs:
- solution: float32 [8, 4, 2, 320, 128], P('stream', 'span')
The draws below stay inside these ranges and needn't reach their ends.
Inputs may be any that keep to these rules, and one draw needn't show every extreme that they name: order[i, j] lists each of the 2 slots of line (i, j) once. `counts`: some line holds 2 live elements and some line 1. `neighbours`: a slot of the same line other than the element's own, or 2 where the face has no in-line neighbour.
All inputs are finite; a program needn't handle non-finite values.
Results may differ from the reference program's by a relative error of at most 0.00075.
Values sent between devices are 32-bit elements; how exact they have to be, the bound alone decides.
No kernel may reach another device: no remote copies, remote signals or barrier semaphores. Data moves between devices by JAX's collectives and lax.ppermute only.
A program may use at most 64 MiB of HBM per device.

```python
import math
from functools import partial
import jax
import jax.numpy as jnp
from jax import lax

B = 320
TF = 80
E = 2
NL = 2
FT = 6
R = 128
SWEEPS = 2
LINES_X = 8
LINES_Z = 4


def draw_inv_blocks(key, part):
    noise = jax.random.normal(key, (LINES_X, LINES_Z, E, B, B), jnp.float32)
    identity_block = jnp.eye(B, dtype=jnp.float32)
    return (0.7 * (identity_block + 0.4 * noise / math.sqrt(B))).astype(jnp.bfloat16)


def draw_lift_ops(key, part):
    noise = jax.random.normal(key, (4, B, TF), jnp.float32)
    face_scales = jnp.array([1.3, 1.3, 0.4, 0.4], jnp.float32)
    return (noise * face_scales[:, None, None] / math.sqrt(TF)).astype(jnp.bfloat16)


def draw_counts(key, part):
    line_total = LINES_X * LINES_Z
    drops = (jax.random.randint(key, (line_total,), 0, 4) == 0).astype(jnp.int32)
    raw_counts = E - drops
    chosen = jax.random.randint(jax.random.fold_in(key, 7), (), 0, line_total)
    step_away = jax.random.randint(jax.random.fold_in(key, 9), (), 1, line_total)
    other = (chosen + step_away) % line_total
    filled = raw_counts.at[chosen].set(E).at[other].set(E - 1)
    return filled.reshape(LINES_X, LINES_Z).astype(jnp.int32)


def draw_neighbours(key, part):
    offset_key = jax.random.fold_in(key, 11)
    absent_key = jax.random.fold_in(key, 13)
    offsets = jax.random.randint(offset_key, (LINES_X, LINES_Z, E, NL), 1, E)
    slot_ids = jnp.arange(E, dtype=jnp.int32)[None, None, :, None]
    targets = (slot_ids + offsets) % E
    absent = jax.random.randint(absent_key, (LINES_X, LINES_Z, E, NL), 0, 4) == 0
    return jnp.where(absent, E, targets).astype(jnp.int32)


def touch_ends(drawn, stream_key, least, high):
    spot = [jax.random.randint(jax.random.fold_in(stream_key, axis), (), 0, length) for axis, length in enumerate(drawn.shape)]
    widest = drawn.shape.index(max(drawn.shape))
    next_to = spot[:widest] + [(spot[widest] + 1) % drawn.shape[widest]] + spot[widest + 1:]
    return drawn.at[tuple(spot)].set(least).at[tuple(next_to)].set(high)


def levels(stream_key, shape, split, smallest, top_value):
    loudness = 1.0
    for dim, shards_of in split:
        steps = jax.random.uniform(jax.random.fold_in(jax.random.fold_in(stream_key, 6), dim), (shards_of,), jnp.float32, smallest / len(split), top_value / len(split))
        loudness = loudness * jnp.repeat(jnp.exp(steps), shape[dim] // shards_of).reshape((-1,) + (1,) * (len(shape) - 1 - dim))
    return loudness


def normal_values(rng, extent, scale, limit, cuts=(), held_as=jnp.bfloat16):
    values = jax.random.normal(rng, extent, jnp.float32) * scale
    if len(cuts) > 0:
        values = levels(rng, extent, cuts, -0.22, 0.18) * values
    return jnp.clip(values, min=-limit, max=limit).astype(held_as)


def setup_inputs(seed: int = 0) -> dict:
    seeds = jax.random.split(jax.random.key(seed), 10)
    rhs = normal_values(seeds[0], (LINES_X, LINES_Z, E, B, R), 1.0, 6.0, ((0, 8), (1, 4)), jnp.float32)
    inv_blocks = draw_inv_blocks(jax.random.fold_in(seeds[9], 71), 0)
    coupling = normal_values(seeds[2], (FT, B, B), (B * 11) ** -0.5, 0.109375)
    trace_ops = normal_values(seeds[3], (4, TF, B), B ** -0.5, 0.3125)
    lift_ops = draw_lift_ops(jax.random.fold_in(seeds[9], 71), 0)
    order = jax.vmap(lambda own: jax.random.permutation(own, E))(jax.random.split(seeds[5], LINES_X * LINES_Z)).reshape((LINES_X, LINES_Z, E)).astype(jnp.int32)
    counts = draw_counts(jax.random.fold_in(seeds[9], 71), 0)
    neighbours = draw_neighbours(jax.random.fold_in(seeds[9], 71), 0)
    face_ids = touch_ends(jax.random.randint(seeds[8], (LINES_X, LINES_Z, E, NL), 0, FT), jax.random.fold_in(seeds[8], 1), 0, FT - 1).astype(jnp.int32)
    return {"rhs": rhs, "inv_blocks": inv_blocks, "coupling": coupling, "trace_ops": trace_ops, "lift_ops": lift_ops, "order": order, "counts": counts, "neighbours": neighbours, "face_ids": face_ids}


HIGH = lax.Precision.HIGHEST


def column_sweep(solution, residual, inverse, order, count, neighbours, face_ids, coupling, backward):
    slot_count = solution.shape[0]
    positions = range(slot_count - 1, -1, -1) if backward else range(slot_count)
    for position in positions:
        slot_index = order[position]
        residual_now = lax.dynamic_index_in_dim(residual, slot_index, 0, keepdims=False)
        for face_index in range(neighbours.shape[1]):
            neighbour_slot = neighbours[slot_index, face_index]
            present = neighbour_slot < slot_count
            neighbour_block = lax.dynamic_index_in_dim(solution, jnp.minimum(neighbour_slot, slot_count - 1), 0, keepdims=False)
            coupling_block = lax.dynamic_index_in_dim(coupling, face_ids[slot_index, face_index], 0, keepdims=False)
            product = jnp.dot(coupling_block, neighbour_block, precision=HIGH)
            residual_now = residual_now - jnp.where(present, product, jnp.zeros_like(product))
        inverse_block = lax.dynamic_index_in_dim(inverse, slot_index, 0, keepdims=False).astype(jnp.float32)
        live_factor = (position < count).astype(jnp.float32)
        updated = jnp.dot(inverse_block, residual_now, precision=HIGH) * live_factor
        solution = lax.dynamic_update_index_in_dim(solution, updated, slot_index, 0)
    return solution


def apply_trace(operator, values):
    return jnp.einsum('tb,...br->...tr', operator, values, precision=HIGH)


def apply_lift(operator, traces):
    return jnp.einsum('bt,...tr->...br', operator, traces, precision=HIGH)


def half_sweep(solution, backward, rhs, inv_blocks, coupling_table, traces_op, lifts, order, counts, neighbours, face_ids):
    left_traces = jnp.roll(apply_trace(traces_op[3], solution), 1, axis=1)
    right_traces = jnp.roll(apply_trace(traces_op[2], solution), -1, axis=1)
    residual_base = rhs - apply_lift(lifts[2], left_traces) - apply_lift(lifts[3], right_traces)
    zero_layer = jnp.zeros_like(left_traces[:1])
    if backward:
        previous = jnp.concatenate([zero_layer, apply_trace(traces_op[1], solution)[:-1]], axis=0)
        residual_base = residual_base - apply_lift(lifts[0], previous)
        inflow_lift = lifts[1]
        outflow_trace = traces_op[0]
    else:
        previous = jnp.concatenate([apply_trace(traces_op[0], solution)[1:], zero_layer], axis=0)
        residual_base = residual_base - apply_lift(lifts[1], previous)
        inflow_lift = lifts[0]
        outflow_trace = traces_op[1]
    line_sweep = jax.vmap(partial(column_sweep, coupling=coupling_table, backward=backward))

    def step(carried, items):
        column, base_column, inverse_column, order_column, count_column, link_column, type_column = items
        residual_column = base_column - apply_lift(inflow_lift, carried)
        updated = line_sweep(column, residual_column, inverse_column, order_column, count_column, link_column, type_column)
        return apply_trace(outflow_trace, updated), updated

    initial = jnp.zeros(left_traces.shape[1:], jnp.float32)
    _, result = lax.scan(step, initial, (solution, residual_base, inv_blocks, order, counts, neighbours, face_ids), reverse=backward)
    return result


def reference(rhs, inv_blocks, coupling, trace_ops, lift_ops, order, counts, neighbours, face_ids):
    coupling_table = coupling.astype(jnp.float32)
    traces_op = trace_ops.astype(jnp.float32)
    lifts = lift_ops.astype(jnp.float32)
    solution = jnp.zeros_like(rhs)
    for sweep_index in range(SWEEPS):
        solution = half_sweep(solution, False, rhs, inv_blocks, coupling_table, traces_op, lifts, order, counts, neighbours, face_ids)
        solution = half_sweep(solution, True, rhs, inv_blocks, coupling_table, traces_op, lifts, order, counts, neighbours, face_ids)
    return solution
```

```python
from functools import partial

import jax
import jax.numpy as jnp
from jax import lax
from jax.experimental import pallas as pl
from jax.experimental.pallas import tpu as pltpu
from jax.sharding import PartitionSpec as P

SWEEPS = 2
LANES = 128
F32 = jnp.float32
BF16 = jnp.bfloat16


def mm(a, b):
    return jnp.dot(a, b, preferred_element_type=F32)


def two(x):
    high = x.astype(BF16)
    low = (x - high.astype(F32)).astype(BF16)
    return high, low


def exact_times(operator, x):
    n = x.shape[1]
    both = mm(operator, jnp.concatenate(two(x), axis=1))
    return both[:, :n] + both[:, n:]


def map_times(high, low, x):
    n = x.shape[1]
    x_high, x_low = two(x)
    both = mm(high, jnp.concatenate([x_high, x_low], axis=1))
    return both[:, :n] + both[:, n:] + mm(low, x_high)


def spread(x, slots, width):
    gap = jnp.zeros((LANES - width, x.shape[1]), x.dtype)
    parts = []
    for s in range(slots):
        parts += [x[s * width : (s + 1) * width], gap]
    return jnp.concatenate(parts, axis=0)


def call(body, outs, ins, scalars=0, scratch=(), flops=0):
    vmem, smem = pl.BlockSpec(memory_space=pltpu.VMEM), pl.BlockSpec(memory_space=pltpu.SMEM)
    moved = sum(x.size * x.dtype.itemsize for x in ins)
    moved += sum(o.size * o.dtype.itemsize for o in outs)
    return pl.pallas_call(
        body,
        out_shape=list(outs),
        in_specs=[smem] * scalars + [vmem] * (len(ins) - scalars),
        out_specs=[vmem] * len(outs),
        scratch_shapes=list(scratch),
        compiler_params=pltpu.CompilerParams(vmem_limit_bytes=24 * 2**20),
        cost_estimate=pl.CostEstimate(flops=flops, bytes_accessed=moved, transcendentals=0),
    )(*ins)


def shape(*dims, dtype=F32):
    return jax.ShapeDtypeStruct(dims, dtype)


def neighbour_sum(slot, links, types, table, read, slots):
    total = None
    for m in range(links.shape[1]):
        n = links[slot, m]
        product = exact_times(table[types[slot, m]], read(jnp.minimum(n, slots - 1)))
        product = jnp.where(n < slots, product, 0.0)
        total = product if total is None else total + product
    return total


def sweep_line(x, residual, inverse, order, count, links, types, table, backward, fresh):
    slots = x.shape[0]
    for step, q in enumerate(reversed(range(slots)) if backward else range(slots)):
        s = order[q]
        rest = residual[s]
        if not (fresh and step == 0):
            rest = rest - neighbour_sum(s, links, types, table, lambda n: x[n], slots)
        x[s] = exact_times(inverse[s], rest) * (q < count).astype(F32)


def line_response(out, lift, inverse, order, count, links, types, table, backward):
    slots = out.shape[0]
    out[...] = jnp.zeros_like(out)
    done = []
    for q in reversed(range(slots)) if backward else range(slots):
        s = order[q]
        live = (q < count).astype(F32)
        out[s, q] = mm(inverse[s], lift) * -live
        if done:
            read = lambda n: jnp.concatenate([out[n, p] for p in done], axis=1)
            rest = neighbour_sum(s, links, types, table, read, slots)
            rest = exact_times(inverse[s], rest) * -live
            for i, p in enumerate(done):
                out[s, p] = rest[:, i * LANES : (i + 1) * LANES]
        done.append(q)


def padded_lift(lift_ref, index, pad):
    pad[...] = jnp.zeros_like(pad)
    pad[:, : lift_ref.shape[2]] = lift_ref[index].astype(F32)
    return pad[...].astype(BF16)


def store_map(out, base, response, trace, order):
    slots, width = response.shape[0], trace.shape[0]
    for p in range(slots):
        f = order[p]
        for s in range(slots):
            row = pl.multiple_of(base + (f * slots + s) * width, 8)
            out[pl.ds(row, width), :] = exact_times(trace, response[s, p])


def first_kernel(order, count, links, types, rhs, inverse, table, traces, lifts,
                 packed, x, response, pad):
    slots, width = x.shape[0], traces.shape[1]
    live = count[0]
    x[...] = jnp.zeros_like(x)
    sweep_line(x, rhs, inverse, order, live, links, types, table, False, True)
    for s in range(slots):
        packed[s * width : (s + 1) * width, :] = exact_times(traces[1], x[s])
    lift = padded_lift(lifts, 0, pad)
    line_response(response, lift, inverse, order, live, links, types, table, False)
    store_map(packed, slots * width, response, traces[1], order)


def side_traces(out, traces, x):
    slots, width = x.shape[0], traces.shape[1]
    for s in range(slots):
        for face in (2, 3):
            out[face - 2, s * width : (s + 1) * width, :] = exact_times(traces[face], x[s])


def side_map(high, low, response, traces, order):
    slots, width = response.shape[0], traces.shape[1]
    for p in range(slots):
        f = order[p]
        for face in (2, 3):
            for s in range(slots):
                a, b = two(exact_times(traces[face], response[s, p]))
                row = ((face - 2) * slots + s) * width
                high[f, row : row + width, :] = a
                low[f, row : row + width, :] = b


def maps_kernel(order, count, links, types, inverse, table, traces, lifts, response, x,
                side_f_high, side_f_low, side_b_high, side_b_low, back_map, side, back, pad):
    live = count[0]
    side_traces(side, traces, x)
    side_map(side_f_high, side_f_low, response, traces, order)
    lift = padded_lift(lifts, 1, pad)
    line_response(back, lift, inverse, order, live, links, types, table, True)
    store_map(back_map, 0, back, traces[0], order)
    side_map(side_b_high, side_b_low, back, traces, order)


def local_kernel(backward, involution, order, count, links, types, rhs, old, inverse, table,
                 traces, lifts, first, second, outflow, side, residual, x):
    slots, width = x.shape[0], traces.shape[1]
    odd = lax.rem(lax.axis_index("span"), 2) if involution else 1
    x[...] = old[...]
    for s in range(slots):
        rows = slice(s * width, (s + 1) * width)
        residual[s] = (
            rhs[s]
            - exact_times(lifts[3 - odd], first[rows, :])
            - exact_times(lifts[2 + odd], second[rows, :])
        )
    sweep_line(x, residual, inverse, order, count[0], links, types, table, backward, False)
    out_trace = traces[0 if backward else 1]
    for s in range(slots):
        outflow[s * width : (s + 1) * width, :] = exact_times(out_trace, x[s])
    side_traces(side, traces, x)


def finish_kernel(backward, order, count, links, types, rhs, residual, old, inflow, inverse,
                  table, lifts, x, rhs_next, rest):
    slots, width = x.shape[0], lifts.shape[2]
    lift = lifts[1 if backward else 0]
    x[...] = old[...]
    for s in range(slots):
        entered = exact_times(lift, inflow[s * width : (s + 1) * width, :])
        rest[s] = residual[s] - entered
        if rhs_next is not None:
            rhs_next[s] = rhs[s] - entered
    sweep_line(x, rest, inverse, order, count[0], links, types, table, backward, False)


def digit_of(size, stride, backward):
    digit = lax.rem(lax.div(lax.axis_index("stream"), stride), size)
    return digit


def source_digit(digit, size, k):
    if size & (size - 1) == 0:
        return digit ^ k
    return lax.rem(digit - k + size, size)


def fold_kernel(size, stride, backward, first, slots, *refs):
    parts, refs = refs[:size], refs[size:]
    if first:
        total, before, high, low, held = refs
    else:
        high, low, total, before, held = refs
    rows = total.shape[0]
    width = rows // slots
    digit = digit_of(size, stride, backward)
    place = size - 1 - digit if backward else digit
    for k, part in enumerate(parts):
        m = source_digit(digit, size, k)
        m = size - 1 - m if backward else m
        held[m] = part[:rows, :]
        if first:
            for f in range(slots):
                base = rows * (1 + f)
                a, b = two(part[base : base + rows, :])
                high[m, f] = a
                low[m, f] = b
    state = held[0]
    below = jnp.zeros_like(state)
    for m in range(1, size):
        below = jnp.where(place == m, state, below)
        state = held[m] + wide_times(high, low, m, state, slots, width)
    total[...] = state
    before[...] = below


def wide(ref, m, slots):
    return jnp.concatenate([ref[m, f] for f in range(slots)], axis=1)


def wide_times(high, low, m, x, slots, width):
    return map_times(wide(high, m, slots), wide(low, m, slots), spread(x, slots, width))


def passage_kernel(size, stride, backward, slots, high, low, pass_high, pass_low, whole):
    rows = high.shape[2]
    width = rows // slots
    digit = digit_of(size, stride, backward)
    place = size - 1 - digit if backward else digit
    row = lax.broadcasted_iota(jnp.int32, (rows, slots * LANES), 0)
    lane = lax.broadcasted_iota(jnp.int32, (rows, slots * LANES), 1)
    state = jnp.zeros((rows, slots * LANES), F32)
    for s in range(slots):
        hit = (row - s * width == lane - s * LANES) & (row >= s * width) & (row < (s + 1) * width)
        state = jnp.where(hit, 1.0, state)
    kept = state
    for m in range(size):
        kept = jnp.where(place == m, state, kept)
        if m < size - 1 or whole is not None:
            state = wide_times(high, low, m, state, slots, width)
    a, b = two(kept)
    for f in range(slots):
        pass_high[0, f] = a[:, f * LANES : (f + 1) * LANES]
        pass_low[0, f] = b[:, f * LANES : (f + 1) * LANES]
        if whole is not None:
            whole[f * rows : (f + 1) * rows, :] = state[:, f * LANES : (f + 1) * LANES]


def enter_kernel(depth, last_stride, backward, involution, slots, *refs):
    befores, refs = refs[:depth], refs[depth:]
    passes, refs = refs[: 2 * depth], refs[2 * depth :]
    arrived, side, high, low, inflow, first, second = refs
    rows = inflow.shape[0]
    width = rows // slots
    if last_stride:
        upper = digit_of(2, last_stride, backward) == (0 if backward else 1)
        state = jnp.where(upper, arrived[:rows, :], 0.0)
    else:
        state = jnp.zeros((rows, inflow.shape[1]), F32)
    for level in reversed(range(depth)):
        state = befores[level][...] + wide_times(
            passes[2 * level], passes[2 * level + 1], 0, state, slots, width
        )
    inflow[...] = state
    if first is None:
        return
    hidden = spread(state, slots, width)
    both = map_times(
        jnp.concatenate([high[f] for f in range(slots)], axis=1),
        jnp.concatenate([low[f] for f in range(slots)], axis=1),
        hidden,
    )
    lower_face = side[0] + both[:rows]
    upper_face = side[1] + both[rows:]
    if involution:
        odd = lax.rem(lax.axis_index("span"), 2) == 1
        first[...] = jnp.where(odd, lower_face, upper_face)
        second[...] = jnp.where(odd, upper_face, lower_face)
    else:
        first[...] = upper_face
        second[...] = lower_face


def levels_of(count):
    sizes, left = [], count
    for factor in (4, 2):
        while left % factor == 0:
            sizes.append(factor)
            left //= factor
    factor = 3
    while left > 1:
        while left % factor == 0:
            sizes.insert(0, factor)
            left //= factor
        factor += 2
    strides, stride = [], 1
    for size in sizes:
        strides.append(stride)
        stride *= size
    return list(zip(sizes, strides))


def exchange(block, axis, size, stride, k):
    pairs = []
    for i in range(lax.axis_size(axis)):
        digit = (i // stride) % size
        target = digit ^ k if size & (size - 1) == 0 else (digit + k) % size
        pairs.append((i, i + (target - digit) * stride))
    return lax.ppermute(block, axis, pairs)


def side_exchange(first, second, involution):
    n = lax.axis_size("span")
    if involution:
        pairs = [(j, j ^ 1) for j in range(n)]
        across = [(j, (j + 1) % n if j % 2 else (j - 1) % n) for j in range(n)]
        second = lax.ppermute(second, "span", across)
        first = lax.ppermute(first, "span", pairs)
        return first, second
    return (
        lax.ppermute(first, "span", [(j, (j + 1) % n) for j in range(n)]),
        lax.ppermute(second, "span", [(j, (j - 1) % n) for j in range(n)]),
    )


def optional(body, at):
    def run(*refs):
        return body(*refs[:at], None, *refs[at:])

    return run


def local(rhs, inv_blocks, coupling, trace_ops, lift_ops, order, counts, neighbours, face_ids):
    source, inverse = rhs[0, 0], inv_blocks[0, 0]
    scalars = (order[0, 0], counts[0], neighbours[0, 0], face_ids[0, 0])
    slots, block, columns = source.shape
    width = trace_ops.shape[1]
    rows = slots * width
    levels = levels_of(lax.axis_size("stream"))
    span = lax.axis_size("span")
    involution = span % 2 == 0 and span > 2

    field = shape(slots, block, columns)
    trace = shape(rows, columns)
    sweep_flops = 2 * slots * 3 * 2 * block * block * columns
    map_shape = shape(rows * slots, LANES)
    side_shape = shape(slots, 2 * rows, LANES, dtype=BF16)
    pad = pltpu.VMEM((block, LANES), F32)

    packed, x_local, response = call(
        first_kernel,
        [shape(rows * (1 + slots), LANES), field, shape(slots, slots, block, LANES)],
        (*scalars, source, inverse, coupling, trace_ops, lift_ops),
        4, [pad], 3 * sweep_flops,
    )
    store = {}

    def maps():
        out = call(
            maps_kernel,
            [side_shape] * 4 + [map_shape, shape(2, rows, columns)],
            (*scalars, inverse, coupling, trace_ops, lift_ops, response, x_local),
            4, [pltpu.VMEM((slots, slots, block, LANES), F32), pad], 6 * sweep_flops,
        )
        store["side", False], store["side", True] = out[0:2], out[2:4]
        store["map"], store["first side"] = out[4], out[5]

    def carried(outflow, backward, whole):
        befores, passes, arrived = [], [], None
        total = outflow
        last_stride = 0
        for level, (size, stride) in enumerate(levels):
            last = level == len(levels) - 1
            if last and size == 2:
                arrived, last_stride = exchange(total, "stream", size, stride, 1), stride
                break
            key = ("fold", backward, level)
            first = key not in store
            if first:
                total = jnp.concatenate([total, whole], axis=0) if level else packed_of(total, whole)
            parts = [total] + [exchange(total, "stream", size, stride, k) for k in range(1, size)]
            held = pltpu.VMEM((size, rows, columns), F32)
            kinds = [shape(size, slots, rows, LANES, dtype=BF16)] * 2
            body = partial(fold_kernel, size, stride, backward, first, slots)
            if first:
                total, before, high, low = call(body, [trace, trace] + kinds, parts, 0, [held], 10**8)
                store[key] = (high, low)
                outs = [shape(1, slots, rows, LANES, dtype=BF16)] * 2
                body = partial(passage_kernel, size, stride, backward, slots)
                if last or (level == len(levels) - 2 and levels[-1][0] == 2):
                    store["pass", backward, level] = call(optional(body, 4), outs, (high, low), 0, (), 10**8)
                else:
                    *passed, whole = call(body, outs + [map_shape], (high, low), 0, (), 10**8)
                    store["pass", backward, level] = passed
            else:
                total, before = call(body, [trace, trace], (*parts, *store[key]), 0, [held], 10**8)
            befores.append(before)
            passes += store["pass", backward, level]
        if arrived is None:
            arrived = total
        return befores, passes, arrived, last_stride

    def packed_of(outflow, whole):
        return outflow if whole is None else jnp.concatenate([outflow, whole], axis=0)

    x = None
    rhs_now = source
    halves = [backward for _ in range(SWEEPS) for backward in (False, True)]
    for number, backward in enumerate(halves):
        final = number == len(halves) - 1
        if number == 0:
            residual, x_old = source, jnp.zeros_like(source)
            befores, passes, arrived, last_stride = carried(packed, backward, None)
            maps()
            side = store["first side"]
        else:
            x_old = x
            outflow, side, residual = call(
                partial(local_kernel, backward, involution),
                [trace, shape(2, rows, columns), field],
                (*scalars, rhs_now, x_old, inverse, coupling, trace_ops, lift_ops, first, second),
                4, [pltpu.VMEM(source.shape, F32)], 2 * sweep_flops,
            )
            befores, passes, arrived, last_stride = carried(outflow, backward, store["map"])
        depth = len(befores)
        body = partial(enter_kernel, depth, last_stride, backward, involution, slots)
        ins = (*befores, *passes, arrived, side, *store["side", backward])
        if final:
            def alone(*refs):
                return body(*refs, None, None)
            (inflow,) = call(alone, [trace], ins, 0, (), 10**8)
        else:
            inflow, first, second = call(body, [trace] * 3, ins, 0, (), 10**8)
            first, second = side_exchange(first, second, involution)
        body = partial(finish_kernel, backward)
        ins = (*scalars, source, residual, x_old, inflow, inverse, coupling, lift_ops)
        scratch = [pltpu.VMEM(source.shape, F32)]
        if final:
            (x,) = call(optional(body, len(ins) + 1), [field], ins, 4, scratch, 2 * sweep_flops)
        else:
            x, rhs_now = call(body, [field, field], ins, 4, scratch, 2 * sweep_flops)
    return x[None, None]


def solution(mesh):
    placed = (
        P("stream", "span", None, None, None),
        P("stream", "span", None, None, None),
        P(),
        P(),
        P(),
        P("stream", "span", None),
        P("stream", "span"),
        P("stream", "span", None, None),
        P("stream", "span", None, None),
    )
    return jax.shard_map(
        local,
        mesh=mesh,
        in_specs=placed,
        out_specs=P("stream", "span", None, None, None),
        check_vma=False,
    )
```

```python
from functools import partial

import jax
import jax.numpy as jnp
from jax import lax
from jax.experimental import pallas as pl
from jax.experimental.pallas import tpu as pltpu
from jax.sharding import PartitionSpec as P

SWEEPS = 2
LANES = 128
F32 = jnp.float32
BF16 = jnp.bfloat16


def mm(a, b):
    return jnp.dot(a, b, preferred_element_type=F32)


def mm_t(a, b):
    return lax.dot_general(a, b, (((1,), (1,)), ((), ())), preferred_element_type=F32)


def two(x):
    high = x.astype(BF16)
    low = (x - high.astype(F32)).astype(BF16)
    return high, low


def exact_times(operator, x):
    n = x.shape[1]
    both = mm(operator, jnp.concatenate(two(x), axis=1))
    return both[:, :n] + both[:, n:]


def map_times(high, low, x):
    n = x.shape[1]
    x_high, x_low = two(x)
    both = mm(high, jnp.concatenate([x_high, x_low], axis=1))
    return both[:, :n] + both[:, n:] + mm(low, x_high)


def pad_rows(x):
    gap = jnp.zeros((LANES - x.shape[0], x.shape[1]), x.dtype)
    return jnp.concatenate([x, gap], axis=0)


def spread(x):
    width = x.shape[0] // 2
    return jnp.concatenate([pad_rows(x[:width]), pad_rows(x[width:])], axis=0)


def pick(flag, yes, no):
    return jnp.where(flag, yes, no)


def by_position(flag, x):
    width = x.shape[0] // 2
    return (
        pad_rows(pick(flag, x[:width], x[width:])),
        pad_rows(pick(flag, x[width:], x[:width])),
    )


def slot_map(flag, first, second, across, backward):
    none = jnp.zeros_like(across)
    if backward:
        lower, upper = pick(flag, none, across), pick(flag, across, none)
    else:
        lower, upper = pick(flag, across, none), pick(flag, none, across)
    return (
        jnp.concatenate([pick(flag, first, second), upper], axis=1),
        jnp.concatenate([lower, pick(flag, second, first)], axis=1),
    )


def pack_map(first, second, across, flag_value):
    width = first.shape[0]
    spare = LANES - width
    lane = lax.broadcasted_iota(jnp.int32, first.shape, 1)
    one = jnp.where(lane >= width, pltpu.roll(across, width, 1), first)
    rest = jnp.where(lane >= width, pltpu.roll(across, width - spare, 1), second)
    return one, jnp.where(lane >= 2 * width - spare, flag_value, rest)


def unpack_map(one, two_):
    width = one.shape[0]
    spare = LANES - width
    lane = lax.broadcasted_iota(jnp.int32, one.shape, 1)
    none = jnp.zeros_like(one)
    first = jnp.where(lane < width, one, none)
    second = jnp.where(lane < width, two_, none)
    across = jnp.where(lane < spare, pltpu.roll(one, LANES - width, 1), none)
    rest = pltpu.roll(two_, LANES - (width - spare), 1)
    across = jnp.where((lane >= spare) & (lane < width), rest, across)
    flag = jnp.broadcast_to(two_[0:1, LANES - 1 : LANES], (1, LANES)) > 0.5
    return first, second, across, flag


def call(body, outs, ins, flops=0, scratch=(), spaces=None):
    vmem = pl.BlockSpec(memory_space=pltpu.VMEM)
    moved = sum(x.size * x.dtype.itemsize for x in ins)
    moved += sum(o.size * o.dtype.itemsize for o in outs)
    return pl.pallas_call(
        body,
        out_shape=list(outs),
        in_specs=spaces or [vmem] * len(ins),
        out_specs=[vmem] * len(outs),
        scratch_shapes=list(scratch),
        compiler_params=pltpu.CompilerParams(vmem_limit_bytes=24 * 2**20),
        cost_estimate=pl.CostEstimate(flops=flops, bytes_accessed=moved, transcendentals=0),
    )(*ins)


def shape(*dims, dtype=F32):
    return jax.ShapeDtypeStruct(dims, dtype)


def pair(*dims):
    return [shape(*dims, dtype=BF16)] * 2


def face(ref, q, f, count=1):
    return ref[q, :, f * LANES : (f + count) * LANES]


def lift_times(high, low, q, f, x, count=1):
    return map_times(face(high, q, f, count), face(low, q, f, count), x)


def joined_coupling(blocks, flags, q):
    total = None
    for m in range(blocks.shape[1]):
        present = flags[2 + q * blocks.shape[1] + m : 3 + q * blocks.shape[1] + m, 0:1]
        block = blocks[q, m].astype(F32) * present
        total = block if total is None else total + block
    return two(total)


def first_kernel(order_in, count_in, links_in, types_in, rhs_in, inverse_in, table_in, traces_in,
                 lifts_in, packed, flags, inverse, blocks, traces, lifts, rhs, now, response,
                 held, order, count, links, types, small, large, table_sems):
    faces = blocks.shape[1]
    width = traces.shape[1]
    scalars = [
        pltpu.make_async_copy(a, b, small.at[i])
        for i, (a, b) in enumerate(
            ((order_in, order), (types_in, types), (links_in, links), (count_in, count))
        )
    ]
    for c in scalars:
        c.start()
    pairs = [(inverse_in, held), (rhs_in, rhs), (traces_in, traces)]
    for f in range(lifts_in.shape[0]):
        pairs.append((lifts_in.at[f], lifts.at[pl.ds(f * LANES, width), :]))
    copies = [pltpu.make_async_copy(a, b, large.at[i]) for i, (a, b) in enumerate(pairs)]
    for c in copies:
        c.start()
    for f in range(lifts_in.shape[0]):
        gap = lifts.at[pl.ds(f * LANES + width, LANES - width), :]
        gap[...] = jnp.zeros(gap.shape, BF16)
    for c in scalars:
        c.wait()
    fetched = {}
    for q in (1, 0):
        for m in range(faces):
            c = pltpu.make_async_copy(
                table_in.at[types[order[q], m]], blocks.at[q, m], table_sems.at[q * faces + m]
            )
            c.start()
            fetched[q, m] = c
    a, b = order[0], order[1]
    alive = (count[0] > 1).astype(F32)
    flags[...] = jnp.zeros_like(flags)
    flags[0:1, :] = jnp.full((1, LANES), (a == 0).astype(F32))
    flags[1:2, :] = jnp.full((1, LANES), alive)
    for q in (0, 1):
        for m in range(faces):
            row = 2 + q * faces + m
            present = (links[order[q], m] < 2).astype(F32)
            flags[row : row + 1, :] = jnp.full((1, LANES), present)
    for c in copies:
        c.wait()
    inverse[0] = held[a]
    inverse[1] = held[b] * alive.astype(BF16)
    head = lifts[0:LANES, :]
    now[0] = exact_times(inverse[0], rhs[a])
    response[0] = mm_t(inverse[0], head)
    response[2] = mm_t(inverse[1], head)
    for m in range(faces):
        fetched[1, m].wait()
    high, low = joined_coupling(blocks, flags, 1)
    met = map_times(high, low, jnp.concatenate([now[0], response[0]], axis=1))
    columns = now.shape[2]
    rest = jnp.concatenate([rhs[b] - met[:, :columns], met[:, columns:]], axis=1)
    rest = exact_times(inverse[1], rest)
    now[1] = rest[:, :columns]
    response[1] = rest[:, columns:]
    shown = exact_times(traces[1], jnp.concatenate([now[0], response[0]], axis=1))
    packed[pl.ds(pl.multiple_of(a * width, 8), width), :] = shown[:, :columns]
    after = jnp.concatenate([now[1], response[1], response[2]], axis=1)
    after = exact_times(traces[1], after)
    packed[pl.ds(pl.multiple_of(b * width, 8), width), :] = after[:, :columns]
    one, rest = pack_map(
        -shown[:, columns:],
        -after[:, columns + LANES :],
        after[:, columns : columns + LANES],
        flags[0:1, :],
    )
    packed[2 * width : 3 * width, :] = one
    packed[3 * width : 4 * width, :] = rest
    for m in range(faces):
        fetched[0, m].wait()


def side_traces(out, traces, flag, first, second):
    width = traces.shape[1]
    n = first.shape[1]
    for f in (2, 3):
        shown = exact_times(traces[f], jnp.concatenate([first, second], axis=1))
        out[f - 2, :width, :] = pick(flag, shown[:, :n], shown[:, n:])
        out[f - 2, width:, :] = pick(flag, shown[:, n:], shown[:, :n])


def store_side_map(high, low, traces, flag, first, second, across, backward):
    width = traces.shape[1]
    for f in (2, 3):
        shown = exact_times(traces[f], jnp.concatenate([first, second, across], axis=1))
        rows = slot_map(
            flag, -shown[:, :LANES], -shown[:, LANES : 2 * LANES], shown[:, 2 * LANES :], backward
        )
        for s in (0, 1):
            place = ((f - 2) * 2 + s) * width
            high[place : place + width, :], low[place : place + width, :] = two(rows[s])


def store_line_map(high, low, flag, first, second, across, backward):
    width = first.shape[0]
    for f in (0, 1):
        lanes = slice(f * LANES, (f + 1) * LANES)
        rows = slot_map(flag, -first[:, lanes], -second[:, lanes], across[:, lanes], backward)
        for s in (0, 1):
            place, held = slice(s * width, (s + 1) * width), slice(2 * f * LANES, 2 * (f + 1) * LANES)
            high[place, held], low[place, held] = two(rows[s])


def maps_kernel(flags, inverse, blocks, traces, lifts, rhs, now, response,
                z, d_high, d_low, e_high, e_low, side, side_high, side_low, back_map,
                q_high, q_low, last_high, last_low):
    flag = flags[0:1, :] > 0.5
    side_traces(side, traces, flag, now[0], now[1])
    store_side_map(
        side_high, side_low, traces, flag, response[0], response[2], response[1], False
    )
    z[0] = now[0]
    z[1] = exact_times(inverse[1], pick(flag, rhs[1], rhs[0]))
    for q in (0, 1):
        d_high[q], d_low[q] = two(mm_t(inverse[q], lifts[...]))
        high, low = joined_coupling(blocks, flags, q)
        e_high[q], e_low[q] = two(mm(inverse[q], high) + mm(inverse[q], low))
    faces = lifts.shape[0] // LANES - 1
    high, low = face(d_high, 1, 1, faces), face(d_low, 1, 1, faces)
    both = mm(e_high[0], jnp.concatenate([high, low], axis=1))
    n = faces * LANES
    across = both[:, :n] + both[:, n:] + mm(e_low[0], high)
    last_high[...], last_low[...] = two(across[:, :LANES])
    shown = []
    for q in (0, 1):
        shown.append(
            mm(traces[0], face(d_high, q, 1, faces)) + mm(traces[0], face(d_low, q, 1, faces))
        )
    shown.append(exact_times(traces[0], across))
    width = traces.shape[1]
    one, rest = pack_map(
        -shown[0][:, :LANES], -shown[1][:, :LANES], shown[2][:, :LANES], flags[0:1, :]
    )
    back_map[:width, :] = one
    back_map[width:, :] = rest
    store_line_map(q_high, q_low, flag, *(s[:, LANES:] for s in shown), True)


def more_maps_kernel(flags, traces, d_high, d_low, e_high, e_low, last_high, last_low,
                     side_high, side_low, q_high, q_low):
    flag = flags[0:1, :] > 0.5

    def joined(q, f, count):
        return face(d_high, q, f, count).astype(F32) + face(d_low, q, f, count).astype(F32)

    across = last_high[...].astype(F32) + last_low[...].astype(F32)
    store_side_map(
        side_high, side_low, traces, flag, joined(0, 1, 1), joined(1, 1, 1), across, True
    )
    high, low = face(d_high, 0, 2, 2), face(d_low, 0, 2, 2)
    both = mm(e_high[1], jnp.concatenate([high, low], axis=1))
    n = 2 * LANES
    across = both[:, :n] + both[:, n:] + mm(e_low[1], high)
    shown = exact_times(
        traces[1], jnp.concatenate([joined(0, 2, 2), joined(1, 2, 2), across], axis=1)
    )
    store_line_map(
        q_high, q_low, flag, shown[:, :n], shown[:, n : 2 * n], shown[:, 2 * n :], False
    )


def prepare_kernel(backward, flags, inflow, line, z, d_high, d_low, e_high, e_low, traces,
                   outflow, field, other):
    p0, p1 = (1, 0) if backward else (0, 1)
    f = 1 if backward else 0
    flag = flags[0:1, :] > 0.5
    entered = by_position(flag, inflow[...])
    width = traces.shape[1]
    lifted = lift_times(d_high, d_low, p0, f, entered[p0])
    y = line[...] - lifted
    start = z[p1] - lift_times(d_high, d_low, p1, f, entered[p1])
    start = start - map_times(e_high[p1], e_low[p1], y)
    field[...] = start
    left = z[p0] - lifted
    other[...] = left
    end = left - map_times(e_high[p0], e_low[p0], start)
    fields = (start, end) if p1 == 0 else (end, start)
    n = start.shape[1]
    shown = exact_times(traces[1 if backward else 0], jnp.concatenate(fields, axis=1))
    outflow[:width, :] = pick(flag, shown[:, :n], shown[:, n:])
    outflow[width:, :] = pick(flag, shown[:, n:], shown[:, :n])


def sides(involution, first, second):
    if not involution:
        return first[...], second[...]
    odd = lax.rem(lax.axis_index("span"), 2) == 1
    return pick(odd, first[...], second[...]), pick(odd, second[...], first[...])


def outflow_kernel(involution, base, q_high, q_low, first, second, outflow):
    arrived = jnp.concatenate([spread(v) for v in sides(involution, first, second)], axis=0)
    outflow[...] = base[...] + map_times(q_high[...], q_low[...], arrived)


def field_kernel(backward, involution, flags, first, second, start, left, d_high, d_low, e_high,
                 e_low, traces, line, second_line, side):
    p0, p1 = (1, 0) if backward else (0, 1)
    flag = flags[0:1, :] > 0.5
    arrived = [by_position(flag, v) for v in sides(involution, first, second)]

    def lifted(q):
        both = jnp.concatenate([v[q] for v in arrived], axis=0)
        return lift_times(d_high, d_low, q, 2, both, 2)

    y0 = start[...] - lifted(p0)
    line[...] = y0
    y1 = left[...] - lifted(p1) - map_times(e_high[p1], e_low[p1], y0)
    if second_line is not None:
        second_line[...] = y1
    if side is not None:
        fields = (y1, y0) if backward else (y0, y1)
        side_traces(side, traces, flag, *fields)


def last_kernel(enter, depth, flags, line, second_line, d_high, d_low, last_high, last_low, *refs):
    out = refs[-1]
    flag = flags[0:1, :] > 0.5
    entered = by_position(flag, enter(*refs[:-1]))
    y1 = second_line[...] + map_times(
        jnp.concatenate([last_high[...], -face(d_high, 0, 1)], axis=1),
        jnp.concatenate([last_low[...], -face(d_low, 0, 1)], axis=1),
        jnp.concatenate([entered[1], entered[0]], axis=0),
    )
    y0 = line[...] - lift_times(d_high, d_low, 1, 1, entered[1])
    out[0] = pick(flag, y1, y0)
    out[1] = pick(flag, y0, y1)


def digit_of(size, stride):
    return lax.rem(lax.div(lax.axis_index("stream"), stride), size)


def source_digit(digit, size, k):
    if size & (size - 1) == 0:
        return digit ^ k
    return lax.rem(digit - k + size, size)


def fold_kernel(size, stride, backward, first, *refs):
    parts, refs = refs[:size], refs[size:]
    if first:
        total, before, high, low, held = refs
    else:
        high, low, total, before, held = refs
    rows = total.shape[0]
    width = rows // 2
    digit = digit_of(size, stride)
    place = size - 1 - digit if backward else digit
    for k, part in enumerate(parts):
        m = source_digit(digit, size, k)
        m = size - 1 - m if backward else m
        held[m] = part[:rows, :]
        if first == "packed":
            a, b, c, flag = unpack_map(part[rows : rows + width, :], part[rows + width :, :])
            for s, row in enumerate(slot_map(flag, a, b, c, backward)):
                high[m, s * width : (s + 1) * width], low[m, s * width : (s + 1) * width] = two(row)
        elif first:
            for f in (0, 1):
                a, b = two(part[rows * (1 + f) : rows * (2 + f), :])
                high[m, :, f * LANES : (f + 1) * LANES] = a
                low[m, :, f * LANES : (f + 1) * LANES] = b
    state = held[0]
    below = jnp.zeros_like(state)
    for m in range(1, size):
        below = jnp.where(place == m, state, below)
        state = held[m] + map_times(high[m], low[m], spread(state))
    total[...] = state
    before[...] = below


def passage_kernel(size, stride, backward, high, low, pass_high, pass_low, whole):
    rows = high.shape[1]
    width = rows // 2
    digit = digit_of(size, stride)
    place = size - 1 - digit if backward else digit
    row = lax.broadcasted_iota(jnp.int32, (rows, 2 * LANES), 0)
    lane = lax.broadcasted_iota(jnp.int32, (rows, 2 * LANES), 1)
    moved = jnp.where(row < width, row, row - width + LANES)
    state = jnp.where(moved == lane, 1.0, 0.0)
    kept = state
    for m in range(size):
        kept = jnp.where(place == m, state, kept)
        if m < size - 1 or whole is not None:
            state = map_times(high[m], low[m], spread(state))
    pass_high[...], pass_low[...] = two(kept)
    if whole is not None:
        whole[:rows, :] = state[:, :LANES]
        whole[rows:, :] = state[:, LANES:]


def inflow_of(depth, last_stride, backward, *refs):
    befores, refs = refs[:depth], refs[depth:]
    passes, arrived = refs[: 2 * depth], refs[2 * depth]
    if last_stride:
        upper = digit_of(2, last_stride) == (0 if backward else 1)
        state = jnp.where(upper, arrived[...], 0.0)
    else:
        state = None
    for level in reversed(range(depth)):
        added = befores[level][...]
        if state is not None:
            high, low = passes[2 * level : 2 * level + 2]
            added = added + map_times(high[...], low[...], spread(state))
        state = added
    return jnp.zeros_like(arrived) if state is None else state


def enter_kernel(enter, involution, high, low, side, *refs):
    inflow, first, second = refs[-3:]
    state = enter(*refs[:-3])
    inflow[...] = state
    rows = state.shape[0]
    both = map_times(high[...], low[...], spread(state))
    lower_face = side[0] + both[:rows]
    upper_face = side[1] + both[rows:]
    if involution:
        odd = lax.rem(lax.axis_index("span"), 2) == 1
        first[...] = pick(odd, lower_face, upper_face)
        second[...] = pick(odd, upper_face, lower_face)
    else:
        first[...] = upper_face
        second[...] = lower_face


def levels_of(count):
    sizes, left = [], count
    for factor in (4, 2):
        while left % factor == 0:
            sizes.append(factor)
            left //= factor
    factor = 3
    while left > 1:
        while left % factor == 0:
            sizes.insert(0, factor)
            left //= factor
        factor += 2
    strides, stride = [], 1
    for size in sizes:
        strides.append(stride)
        stride *= size
    return list(zip(sizes, strides))


def exchange(block, axis, size, stride, k):
    pairs = []
    for i in range(lax.axis_size(axis)):
        digit = (i // stride) % size
        target = digit ^ k if size & (size - 1) == 0 else (digit + k) % size
        pairs.append((i, i + (target - digit) * stride))
    return lax.ppermute(block, axis, pairs)


def side_exchange(first, second, involution):
    n = lax.axis_size("span")
    if involution:
        pairs = [(j, j ^ 1) for j in range(n)]
        across = [(j, (j + 1) % n if j % 2 else (j - 1) % n) for j in range(n)]
        second = lax.ppermute(second, "span", across)
        first = lax.ppermute(first, "span", pairs)
        return first, second
    return (
        lax.ppermute(first, "span", [(j, (j + 1) % n) for j in range(n)]),
        lax.ppermute(second, "span", [(j, (j - 1) % n) for j in range(n)]),
    )


def local(rhs, inv_blocks, coupling, trace_ops, lift_ops, order, counts, neighbours, face_ids):
    source, inverse_in = rhs[0, 0], inv_blocks[0, 0]
    slots, block, columns = source.shape
    faces, width = trace_ops.shape[:2]
    links = neighbours.shape[-1]
    rows = 2 * width
    if slots != 2 or columns % LANES or 3 * width >= 2 * LANES:
        raise ValueError("unsupported sizes")
    levels = levels_of(lax.axis_size("stream"))
    span = lax.axis_size("span")
    involution = span % 2 == 0 and span > 2

    field, trace = shape(block, columns), shape(rows, columns)
    unit = 2 * block * block * LANES
    hbm = pl.BlockSpec(memory_space=pl.ANY)
    ins = (order[0, 0], counts[0], neighbours[0, 0], face_ids[0, 0], source, inverse_in, coupling,
           trace_ops, jnp.swapaxes(lift_ops, 1, 2))
    ins = tuple(
        x if x.size == 1 else pltpu.with_memory_space_constraint(x, pltpu.HBM) for x in ins
    )
    packed, flags, inverse, blocks, traces, lifts, held_rhs, now, response = call(
        first_kernel,
        [
            shape(2 * rows, LANES),
            shape(8 * -(-(2 + 2 * links) // 8), LANES),
            shape(2, block, block, dtype=BF16),
            shape(2, links, block, block, dtype=BF16),
            shape(faces, width, block, dtype=BF16),
            shape(faces * LANES, block, dtype=BF16),
            shape(2, block, columns),
            shape(2, block, columns),
            shape(3, block, LANES),
        ],
        ins,
        20 * unit,
        [
            pltpu.VMEM((2, block, block), BF16),
            *(pltpu.SMEM(x.shape, jnp.int32) for x in ins[:4]),
            pltpu.SemaphoreType.DMA((4,)),
            pltpu.SemaphoreType.DMA((3 + faces,)),
            pltpu.SemaphoreType.DMA((2 * links,)),
        ],
        [hbm] * len(ins),
    )
    table, square = pair(2, block, faces * LANES), pair(2, block, block)
    side_pair, line_pair = pair(2 * rows, 2 * LANES), pair(rows, 4 * LANES)
    store = {}

    def maps():
        return call(
            maps_kernel,
            [shape(2, block, columns), *table, *square, shape(2, rows, columns), *side_pair,
             shape(rows, LANES), *line_pair, *pair(block, LANES)],
            (flags, inverse, blocks, traces, lifts, held_rhs, now, response),
            40 * unit,
        )

    def more_maps():
        return call(
            more_maps_kernel,
            [*side_pair, *line_pair],
            (flags, traces, *store["d"], *store["e"], *store["last"]),
            16 * unit,
        )

    def carried(total, backward, whole, beside, later):
        befores, passes, arrived, done = [], [], total, None
        last_stride = 0
        for level, (size, stride) in enumerate(levels):
            last = level == len(levels) - 1
            if last and size == 2:
                arrived, last_stride = exchange(total, "stream", size, stride, 1), stride
                break
            key = ("fold", backward, level)
            first = key not in store
            if first:
                first = "whole" if level else "packed"
                if whole is not None:
                    total = jnp.concatenate([total, whole], axis=0)
            parts = [exchange(total, "stream", size, stride, k) for k in reversed(range(1, size))]
            parts = [total] + parts[::-1]
            if level == 0:
                parts, done = lax.optimization_barrier((parts, beside()))
            held = pltpu.VMEM((size, rows, columns), F32)
            body = partial(fold_kernel, size, stride, backward, first)
            if first:
                kinds = pair(size, rows, 2 * LANES)
                total, before, *store[key] = call(body, [trace, trace] + kinds, parts, unit, [held])
                body = partial(passage_kernel, size, stride, backward)
                if last or (level == len(levels) - 2 and levels[-1][0] == 2):
                    body, outs = partial(lambda f, *refs: f(*refs, None), body), []
                else:
                    outs = [shape(2 * rows, LANES)]
                outs = pair(rows, 2 * LANES) + outs
                high, low, *whole = call(body, outs, tuple(store[key]), 2 * unit)
                store["pass", backward, level] = (high, low)
                whole = whole[0] if whole else None
            else:
                total, before = call(body, [trace, trace], (*parts, *store[key]), unit, [held])
            befores.append(before)
            passes += store["pass", backward, level]
        done = beside() if done is None else done
        if later is not None:
            arrived, more = lax.optimization_barrier((arrived, later(done)))
            done = (done, more)
        depth = len(befores)
        return partial(inflow_of, depth, last_stride, backward), (*befores, *passes, arrived), done

    halves = [backward for _ in range(SWEEPS) for backward in (False, True)]
    for number, backward in enumerate(halves):
        final = number == len(halves) - 1
        if number == 0:
            enter, parts, done = carried(packed, backward, None, maps, None)
            store["z"], store["d"], store["e"], side = done[0], done[1:3], done[3:5], done[5]
            store["side", False], store["map"], store["line", True] = done[6:8], done[8], done[9:11]
            store["last"] = done[11:13]
            line = now[0]
        else:
            (outflow,) = call(
                partial(outflow_kernel, involution),
                [trace],
                (base, *store["line", backward], first, second),
                unit,
            )
            body = partial(field_kernel, backward, involution)
            outs = [field, field] if final else [field, shape(2, rows, columns)]
            ins = (flags, first, second, start, left, *store["d"], *store["e"], traces)
            cut = len(ins) + (2 if final else 1)
            body = partial(lambda f, n, *refs: f(*refs[:n], None, *refs[n:]), body, cut)
            later = (lambda _: more_maps()) if number == 1 else None
            beside = partial(call, body, outs, ins, 14 * unit)
            enter, parts, done = carried(outflow, backward, store["map"], beside, later)
            if later:
                done, more = done
                store["side", True], store["line", False] = more[:2], more[2:]
            line, side = done
        if final:
            ins = (flags, line, side, *store["d"], *store["last"], *parts)
            (x,) = call(partial(last_kernel, enter, len(parts)), [shape(2, block, columns)], ins, 4 * unit)
            break
        inflow, first, second = call(
            partial(enter_kernel, enter, involution),
            [trace] * 3,
            (*store["side", backward], side, *parts),
            unit,
        )
        first, second = side_exchange(first, second, involution)
        base, start, left = call(
            partial(prepare_kernel, backward),
            [trace, field, field],
            (flags, inflow, line, store["z"], *store["d"], *store["e"], traces),
            14 * unit,
        )
    return x[None, None]


def solution(mesh):
    placed = (
        P("stream", "span", None, None, None),
        P("stream", "span", None, None, None),
        P(),
        P(),
        P(),
        P("stream", "span", None),
        P("stream", "span"),
        P("stream", "span", None, None),
        P("stream", "span", None, None),
    )
    return jax.shard_map(
        local,
        mesh=mesh,
        in_specs=placed,
        out_specs=P("stream", "span", None, None, None),
        check_vma=False,
    )
```

```python
from functools import partial

import jax
import jax.numpy as jnp
from jax import lax
from jax.experimental import pallas as pl
from jax.experimental.pallas import tpu as pltpu
from jax.sharding import PartitionSpec as P

SWEEPS = 2
LANES = 128
F32 = jnp.float32
BF16 = jnp.bfloat16


def mm(a, b):
    return jnp.dot(a, b, preferred_element_type=F32)


def mm_t(a, b):
    return lax.dot_general(a, b, (((1,), (1,)), ((), ())), preferred_element_type=F32)


def two(x):
    high = x.astype(BF16)
    low = (x - high.astype(F32)).astype(BF16)
    return high, low


def exact_times(operator, x):
    n = x.shape[1]
    both = mm(operator, jnp.concatenate(two(x), axis=1))
    return both[:, :n] + both[:, n:]


def map_times(high, low, x):
    n = x.shape[1]
    x_high, x_low = two(x)
    both = mm(high, jnp.concatenate([x_high, x_low], axis=1))
    return both[:, :n] + both[:, n:] + mm(low, x_high)


def pad_rows(x):
    gap = jnp.zeros((LANES - x.shape[0], x.shape[1]), x.dtype)
    return jnp.concatenate([x, gap], axis=0)


def spread(x):
    width = x.shape[0] // 2
    return jnp.concatenate([pad_rows(x[:width]), pad_rows(x[width:])], axis=0)


def pick(flag, yes, no):
    return jnp.where(flag, yes, no)


def by_position(flag, x):
    width = x.shape[0] // 2
    return (
        pad_rows(pick(flag, x[:width], x[width:])),
        pad_rows(pick(flag, x[width:], x[:width])),
    )


def slot_map(flag, first, second, across, backward):
    none = jnp.zeros_like(across)
    if backward:
        lower, upper = pick(flag, none, across), pick(flag, across, none)
    else:
        lower, upper = pick(flag, across, none), pick(flag, none, across)
    return (
        jnp.concatenate([pick(flag, first, second), upper], axis=1),
        jnp.concatenate([lower, pick(flag, second, first)], axis=1),
    )


def pack_map(first, second, across, flag_value):
    width = first.shape[0]
    spare = LANES - width
    lane = lax.broadcasted_iota(jnp.int32, first.shape, 1)
    one = jnp.where(lane >= width, pltpu.roll(across, width, 1), first)
    rest = jnp.where(lane >= width, pltpu.roll(across, width - spare, 1), second)
    return one, jnp.where(lane >= 2 * width - spare, flag_value, rest)


def unpack_map(one, two_):
    width = one.shape[0]
    spare = LANES - width
    lane = lax.broadcasted_iota(jnp.int32, one.shape, 1)
    none = jnp.zeros_like(one)
    first = jnp.where(lane < width, one, none)
    second = jnp.where(lane < width, two_, none)
    across = jnp.where(lane < spare, pltpu.roll(one, LANES - width, 1), none)
    rest = pltpu.roll(two_, LANES - (width - spare), 1)
    across = jnp.where((lane >= spare) & (lane < width), rest, across)
    flag = jnp.broadcast_to(two_[0:1, LANES - 1 : LANES], (1, LANES)) > 0.5
    return first, second, across, flag


def call(body, outs, ins, flops=0, scratch=(), spaces=None):
    vmem = pl.BlockSpec(memory_space=pltpu.VMEM)
    moved = sum(x.size * x.dtype.itemsize for x in ins)
    moved += sum(o.size * o.dtype.itemsize for o in outs)
    return pl.pallas_call(
        body,
        out_shape=list(outs),
        in_specs=spaces or [vmem] * len(ins),
        out_specs=[vmem] * len(outs),
        scratch_shapes=list(scratch),
        compiler_params=pltpu.CompilerParams(vmem_limit_bytes=24 * 2**20),
        cost_estimate=pl.CostEstimate(flops=flops, bytes_accessed=moved, transcendentals=0),
    )(*ins)


def shape(*dims, dtype=F32):
    return jax.ShapeDtypeStruct(dims, dtype)


def pair(*dims):
    return [shape(*dims, dtype=BF16)] * 2


def face(ref, q, f, count=1):
    return ref[q, :, f * LANES : (f + count) * LANES]


def lift_times(high, low, q, f, x, count=1):
    return map_times(face(high, q, f, count), face(low, q, f, count), x)


def joined_coupling(blocks, flags, q):
    total = None
    for m in range(blocks.shape[1]):
        present = flags[2 + q * blocks.shape[1] + m : 3 + q * blocks.shape[1] + m, 0:1]
        block = blocks[q, m].astype(F32) * present
        total = block if total is None else total + block
    return two(total)


def first_kernel(order_in, count_in, links_in, types_in, rhs_in, inverse_in, table_in, traces_in,
                 lifts_in, packed, flags, inverse, blocks, traces, lifts, rhs, now, response,
                 held, order, count, links, types, small, large, table_sems):
    faces = blocks.shape[1]
    width = traces.shape[1]
    scalars = [
        pltpu.make_async_copy(a, b, small.at[i])
        for i, (a, b) in enumerate(
            ((order_in, order), (types_in, types), (links_in, links), (count_in, count))
        )
    ]
    for c in scalars:
        c.start()
    pairs = [(inverse_in, held), (rhs_in, rhs), (traces_in, traces)]
    for f in range(lifts_in.shape[0]):
        pairs.append((lifts_in.at[f], lifts.at[pl.ds(f * LANES, width), :]))
    copies = [pltpu.make_async_copy(a, b, large.at[i]) for i, (a, b) in enumerate(pairs)]
    for c in copies:
        c.start()
    for f in range(lifts_in.shape[0]):
        gap = lifts.at[pl.ds(f * LANES + width, LANES - width), :]
        gap[...] = jnp.zeros(gap.shape, BF16)
    for c in scalars:
        c.wait()
    fetched = {}
    for q in (1, 0):
        for m in range(faces):
            c = pltpu.make_async_copy(
                table_in.at[types[order[q], m]], blocks.at[q, m], table_sems.at[q * faces + m]
            )
            c.start()
            fetched[q, m] = c
    a, b = order[0], order[1]
    alive = (count[0] > 1).astype(F32)
    flags[...] = jnp.zeros_like(flags)
    flags[0:1, :] = jnp.full((1, LANES), (a == 0).astype(F32))
    flags[1:2, :] = jnp.full((1, LANES), alive)
    for q in (0, 1):
        for m in range(faces):
            row = 2 + q * faces + m
            present = (links[order[q], m] < 2).astype(F32)
            flags[row : row + 1, :] = jnp.full((1, LANES), present)
    for c in copies:
        c.wait()
    inverse[0] = held[a]
    inverse[1] = held[b] * alive.astype(BF16)
    head = lifts[0:LANES, :]
    now[0] = exact_times(inverse[0], rhs[a])
    response[0] = mm_t(inverse[0], head)
    response[2] = mm_t(inverse[1], head)
    for m in range(faces):
        fetched[1, m].wait()
    high, low = joined_coupling(blocks, flags, 1)
    met = map_times(high, low, jnp.concatenate([now[0], response[0]], axis=1))
    columns = now.shape[2]
    rest = jnp.concatenate([rhs[b] - met[:, :columns], met[:, columns:]], axis=1)
    rest = exact_times(inverse[1], rest)
    now[1] = rest[:, :columns]
    response[1] = rest[:, columns:]
    shown = exact_times(traces[1], jnp.concatenate([now[0], response[0]], axis=1))
    packed[pl.ds(pl.multiple_of(a * width, 8), width), :] = shown[:, :columns]
    after = jnp.concatenate([now[1], response[1], response[2]], axis=1)
    after = exact_times(traces[1], after)
    packed[pl.ds(pl.multiple_of(b * width, 8), width), :] = after[:, :columns]
    one, rest = pack_map(
        -shown[:, columns:],
        -after[:, columns + LANES :],
        after[:, columns : columns + LANES],
        flags[0:1, :],
    )
    packed[2 * width : 3 * width, :] = one
    packed[3 * width : 4 * width, :] = rest
    for m in range(faces):
        fetched[0, m].wait()


def side_traces(out, traces, flag, first, second):
    width = traces.shape[1]
    n = first.shape[1]
    for f in (2, 3):
        shown = exact_times(traces[f], jnp.concatenate([first, second], axis=1))
        out[f - 2, :width, :] = pick(flag, shown[:, :n], shown[:, n:])
        out[f - 2, width:, :] = pick(flag, shown[:, n:], shown[:, :n])


def store_side_map(high, low, traces, flag, first, second, across, backward):
    width = traces.shape[1]
    for f in (2, 3):
        shown = exact_times(traces[f], jnp.concatenate([first, second, across], axis=1))
        rows = slot_map(
            flag, -shown[:, :LANES], -shown[:, LANES : 2 * LANES], shown[:, 2 * LANES :], backward
        )
        for s in (0, 1):
            place = ((f - 2) * 2 + s) * width
            high[place : place + width, :], low[place : place + width, :] = two(rows[s])


def store_line_map(high, low, flag, first, second, across, backward):
    width = first.shape[0]
    for f in (0, 1):
        lanes = slice(f * LANES, (f + 1) * LANES)
        rows = slot_map(flag, -first[:, lanes], -second[:, lanes], across[:, lanes], backward)
        for s in (0, 1):
            place, held = slice(s * width, (s + 1) * width), slice(2 * f * LANES, 2 * (f + 1) * LANES)
            high[place, held], low[place, held] = two(rows[s])


def maps_kernel(flags, inverse, blocks, traces, lifts, rhs, now, response,
                z, d_high, d_low, e_high, e_low, side, side_high, side_low, back_map,
                q_high, q_low, last_high, last_low):
    flag = flags[0:1, :] > 0.5
    side_traces(side, traces, flag, now[0], now[1])
    store_side_map(
        side_high, side_low, traces, flag, response[0], response[2], response[1], False
    )
    z[0] = now[0]
    z[1] = exact_times(inverse[1], pick(flag, rhs[1], rhs[0]))
    for q in (0, 1):
        d_high[q], d_low[q] = two(mm_t(inverse[q], lifts[...]))
        high, low = joined_coupling(blocks, flags, q)
        e_high[q], e_low[q] = two(mm(inverse[q], high) + mm(inverse[q], low))
    faces = lifts.shape[0] // LANES - 1
    high, low = face(d_high, 1, 1, faces), face(d_low, 1, 1, faces)
    both = mm(e_high[0], jnp.concatenate([high, low], axis=1))
    n = faces * LANES
    across = both[:, :n] + both[:, n:] + mm(e_low[0], high)
    last_high[...], last_low[...] = two(across[:, :LANES])
    shown = []
    for q in (0, 1):
        shown.append(
            mm(traces[0], face(d_high, q, 1, faces)) + mm(traces[0], face(d_low, q, 1, faces))
        )
    shown.append(exact_times(traces[0], across))
    width = traces.shape[1]
    one, rest = pack_map(
        -shown[0][:, :LANES], -shown[1][:, :LANES], shown[2][:, :LANES], flags[0:1, :]
    )
    back_map[:width, :] = one
    back_map[width:, :] = rest
    store_line_map(q_high, q_low, flag, *(s[:, LANES:] for s in shown), True)


def more_maps_kernel(flags, traces, d_high, d_low, e_high, e_low, last_high, last_low,
                     side_high, side_low, q_high, q_low):
    flag = flags[0:1, :] > 0.5

    def joined(q, f, count):
        return face(d_high, q, f, count).astype(F32) + face(d_low, q, f, count).astype(F32)

    across = last_high[...].astype(F32) + last_low[...].astype(F32)
    store_side_map(
        side_high, side_low, traces, flag, joined(0, 1, 1), joined(1, 1, 1), across, True
    )
    high, low = face(d_high, 0, 2, 2), face(d_low, 0, 2, 2)
    both = mm(e_high[1], jnp.concatenate([high, low], axis=1))
    n = 2 * LANES
    across = both[:, :n] + both[:, n:] + mm(e_low[1], high)
    shown = exact_times(
        traces[1], jnp.concatenate([joined(0, 2, 2), joined(1, 2, 2), across], axis=1)
    )
    store_line_map(
        q_high, q_low, flag, shown[:, :n], shown[:, n : 2 * n], shown[:, 2 * n :], False
    )


def prepare_kernel(backward, flags, inflow, line, z, d_high, d_low, e_high, e_low, traces,
                   outflow, field, other):
    p0, p1 = (1, 0) if backward else (0, 1)
    f = 1 if backward else 0
    flag = flags[0:1, :] > 0.5
    entered = by_position(flag, inflow[...])
    width = traces.shape[1]
    lifted = lift_times(d_high, d_low, p0, f, entered[p0])
    y = line[...] - lifted
    start = z[p1] - lift_times(d_high, d_low, p1, f, entered[p1])
    start = start - map_times(e_high[p1], e_low[p1], y)
    field[...] = start
    left = z[p0] - lifted
    other[...] = left
    end = left - map_times(e_high[p0], e_low[p0], start)
    fields = (start, end) if p1 == 0 else (end, start)
    n = start.shape[1]
    shown = exact_times(traces[1 if backward else 0], jnp.concatenate(fields, axis=1))
    outflow[:width, :] = pick(flag, shown[:, :n], shown[:, n:])
    outflow[width:, :] = pick(flag, shown[:, n:], shown[:, :n])


def sides(involution, first, second):
    if not involution:
        return first[...], second[...]
    odd = lax.rem(lax.axis_index("span"), 2) == 1
    return pick(odd, first[...], second[...]), pick(odd, second[...], first[...])


def outflow_kernel(involution, base, q_high, q_low, first, second, outflow):
    arrived = jnp.concatenate([spread(v) for v in sides(involution, first, second)], axis=0)
    outflow[...] = base[...] + map_times(q_high[...], q_low[...], arrived)


def field_kernel(backward, involution, flags, first, second, start, left, d_high, d_low, e_high,
                 e_low, traces, line, second_line, side):
    p0, p1 = (1, 0) if backward else (0, 1)
    flag = flags[0:1, :] > 0.5
    arrived = [by_position(flag, v) for v in sides(involution, first, second)]

    def lifted(q):
        both = jnp.concatenate([v[q] for v in arrived], axis=0)
        return lift_times(d_high, d_low, q, 2, both, 2)

    y0 = start[...] - lifted(p0)
    line[...] = y0
    y1 = left[...] - lifted(p1) - map_times(e_high[p1], e_low[p1], y0)
    if second_line is not None:
        second_line[...] = y1
    if side is not None:
        fields = (y1, y0) if backward else (y0, y1)
        side_traces(side, traces, flag, *fields)


def last_response_kernel(depth, flags, d_high, d_low, last_high, last_low, *refs):
    passes, (high, low, far_high, far_low) = refs[:-4], refs[-4:]
    flag = flags[0:1, :] > 0.5
    none = jnp.zeros((d_high.shape[1], LANES), F32)

    def joined(h, l):
        return h.astype(F32) + l.astype(F32)

    own = -joined(face(d_high, 0, 1), face(d_low, 0, 1))
    other = -joined(face(d_high, 1, 1), face(d_low, 1, 1))
    across = joined(last_high[...], last_low[...])
    rows = slot_map(flag, own, other, across, True)
    for s in (0, 1):
        high[s], low[s] = two(rows[s])
        far_high[s], far_low[s] = two(through(high[s], low[s], depth, passes))


def last_base_kernel(flags, line, second_line, high, low, inflow, out):
    flag = flags[0:1, :] > 0.5
    entered = spread(inflow[...])
    out[0] = pick(flag, second_line[...], line[...]) + map_times(high[0], low[0], entered)
    out[1] = pick(flag, line[...], second_line[...]) + map_times(high[1], low[1], entered)


def last_kernel(stride, backward, base, high, low, arrived, out):
    entered = spread(last_arrived(stride, backward, arrived))
    for s in (0, 1):
        out[s] = base[s] + map_times(high[s], low[s], entered)


def digit_of(size, stride):
    return lax.rem(lax.div(lax.axis_index("stream"), stride), size)


def place_of(size, stride, backward):
    digit = digit_of(size, stride)
    return size - 1 - digit if backward else digit


def source_place(size, stride, backward, i):
    digit, k = digit_of(size, stride), (size - i) % size
    m = digit ^ k if size & (size - 1) == 0 else lax.rem(digit - k + size, size)
    return size - 1 - m if backward else m


def store_packed(high, low, m, packed, backward):
    width = packed.shape[0] // 2
    a, b, c, flag = unpack_map(packed[:width], packed[width:])
    for s, row in enumerate(slot_map(flag, a, b, c, backward)):
        high[m, s * width : (s + 1) * width], low[m, s * width : (s + 1) * width] = two(row)


def in_turn(size, place, values, high, low):
    state = values[0]
    below = jnp.zeros_like(state)
    for m in range(1, size):
        below = jnp.where(place == m, state, below)
        if m < size:
            state = values[m] + map_times(high[m], low[m], spread(state))
    return state, below


def fold_kernel(size, stride, backward, first, *refs):
    parts, refs = refs[:size], refs[size:]
    if first:
        total, before, high, low, held = refs
    else:
        high, low, total, before, held = refs
    rows = total.shape[0]
    for i, part in enumerate(parts):
        m = source_place(size, stride, backward, i)
        held[m] = part[:rows, :]
        if first == "packed":
            store_packed(high, low, m, part[rows:, :], backward)
        elif first:
            for f in (0, 1):
                a, b = two(part[rows * (1 + f) : rows * (2 + f), :])
                high[m, :, f * LANES : (f + 1) * LANES] = a
                low[m, :, f * LANES : (f + 1) * LANES] = b
    place = place_of(size, stride, backward)
    total[...], before[...] = in_turn(size, place, held, high, low)


def unpack_kernel(size, stride, backward, *refs):
    parts, (high, low) = refs[:size], refs[size:]
    for i, part in enumerate(parts):
        store_packed(high, low, source_place(size, stride, backward, i), part[...], backward)


def total_kernel(size, stride, backward, *refs):
    parts, (high, low, total, held) = refs[:size], refs[size:]
    for i, part in enumerate(parts):
        held[source_place(size, stride, backward, i)] = part[...]
    below = jnp.concatenate([spread(held[m]) for m in range(size - 1)], axis=0)
    total[...] = held[size - 1] + map_times(high[...], low[...], below)


def before_kernel(size, stride, backward, held, high, low, before):
    place = place_of(size, stride, backward)
    _, before[...] = in_turn(size, place, held, high, low)


def suffix_kernel(size, high, low, out_high, out_low):
    state_high, state_low = high[size - 1], low[size - 1]
    for m in reversed(range(size - 1)):
        lanes = slice(2 * LANES * m, 2 * LANES * (m + 1))
        out_high[:, lanes], out_low[:, lanes] = state_high, state_low
        if m:
            inner = high[m].astype(F32) + low[m].astype(F32)
            state_high, state_low = two(map_times(state_high, state_low, spread(inner)))


def passage_kernel(size, stride, backward, high, low, pass_high, pass_low, whole):
    rows = high.shape[1]
    width = rows // 2
    place = place_of(size, stride, backward)
    row = lax.broadcasted_iota(jnp.int32, (rows, 2 * LANES), 0)
    lane = lax.broadcasted_iota(jnp.int32, (rows, 2 * LANES), 1)
    moved = jnp.where(row < width, row, row - width + LANES)
    state = jnp.where(moved == lane, 1.0, 0.0)
    kept = state
    for m in range(size):
        kept = jnp.where(place == m, state, kept)
        if m < size - 1 or whole is not None:
            if m:
                state = map_times(high[m], low[m], spread(state))
            else:
                state = high[0].astype(F32) + low[0].astype(F32)
    pass_high[...], pass_low[...] = two(kept)
    if whole is not None:
        whole[:rows, :] = state[:, :LANES]
        whole[rows:, :] = state[:, LANES:]


def through(high, low, depth, passes):
    state = None
    for level in range(depth):
        if state is not None:
            high, low = two(state)
        inner = passes[2 * level][...].astype(F32) + passes[2 * level + 1][...].astype(F32)
        state = map_times(high, low, spread(inner))
    return high.astype(F32) + low.astype(F32) if state is None else state


def join_kernel(depth, side_high, side_low, *refs):
    passes, (high, low) = refs[:-2], refs[-2:]
    rows = side_high.shape[0]
    high[:rows], low[:rows] = two(through(side_high[...], side_low[...], depth, passes))
    if depth == 1:
        high[rows:], low[rows:] = passes[0][...], passes[1][...]
    else:
        high[rows:], low[rows:] = two(through(passes[0][...], passes[1][...], depth - 1, passes[2:]))


def base_kernel(depth, *refs):
    befores, refs = refs[:depth], refs[depth:]
    passes, refs = refs[: 2 * depth], refs[2 * depth :]
    side, high, low, base, inflow = refs
    state = befores[depth - 1][...]
    for level in reversed(range(depth - 1)):
        inner = map_times(passes[2 * level][...], passes[2 * level + 1][...], spread(state))
        state = befores[level][...] + inner
    inflow[...] = state
    if base is not None:
        both = map_times(high[...], low[...], spread(state))
        rows = state.shape[0]
        base[0] = side[0] + both[:rows]
        base[1] = side[1] + both[rows:]


def last_arrived(stride, backward, arrived):
    if not stride:
        return jnp.zeros(arrived.shape, F32)
    upper = digit_of(2, stride) == (0 if backward else 1)
    return jnp.where(upper, arrived[...], 0.0)


def enter_kernel(stride, backward, involution, base, before, high, low, arrived,
                 inflow, first, second):
    rows = inflow.shape[0]
    entered = spread(last_arrived(stride, backward, arrived))
    added = map_times(high[...], low[...], entered)
    inflow[...] = before[...] + added[2 * rows :]
    lower_face = base[0] + added[:rows]
    upper_face = base[1] + added[rows : 2 * rows]
    if involution:
        odd = lax.rem(lax.axis_index("span"), 2) == 1
        first[...] = pick(odd, lower_face, upper_face)
        second[...] = pick(odd, upper_face, lower_face)
    else:
        first[...] = upper_face
        second[...] = lower_face


def levels_of(count):
    sizes, left = [], count
    for factor in (4, 2):
        while left % factor == 0:
            sizes.append(factor)
            left //= factor
    factor = 3
    while left > 1:
        while left % factor == 0:
            sizes.insert(0, factor)
            left //= factor
        factor += 2
    strides, stride = [], 1
    for size in sizes:
        strides.append(stride)
        stride *= size
    return list(zip(sizes, strides))


def exchange(block, axis, size, stride, k):
    pairs = []
    for i in range(lax.axis_size(axis)):
        digit = (i // stride) % size
        target = digit ^ k if size & (size - 1) == 0 else (digit + k) % size
        pairs.append((i, i + (target - digit) * stride))
    return lax.ppermute(block, axis, pairs)


def side_exchange(first, second, involution):
    n = lax.axis_size("span")
    if involution:
        pairs = [(j, j ^ 1) for j in range(n)]
        across = [(j, (j + 1) % n if j % 2 else (j - 1) % n) for j in range(n)]
        second = lax.ppermute(second, "span", across)
        first = lax.ppermute(first, "span", pairs)
        return first, second
    return (
        lax.ppermute(first, "span", [(j, (j + 1) % n) for j in range(n)]),
        lax.ppermute(second, "span", [(j, (j - 1) % n) for j in range(n)]),
    )


def local(rhs, inv_blocks, coupling, trace_ops, lift_ops, order, counts, neighbours, face_ids):
    source, inverse_in = rhs[0, 0], inv_blocks[0, 0]
    slots, block, columns = source.shape
    faces, width = trace_ops.shape[:2]
    links = neighbours.shape[-1]
    rows = 2 * width
    if slots != 2 or columns % LANES or 3 * width >= 2 * LANES:
        raise ValueError("unsupported sizes")
    levels = levels_of(lax.axis_size("stream"))
    span = lax.axis_size("span")
    involution = span % 2 == 0 and span > 2

    field, trace = shape(block, columns), shape(rows, columns)
    unit = 2 * block * block * LANES
    hbm = pl.BlockSpec(memory_space=pl.ANY)
    ins = (order[0, 0], counts[0], neighbours[0, 0], face_ids[0, 0], source, inverse_in, coupling,
           trace_ops, jnp.swapaxes(lift_ops, 1, 2))
    ins = tuple(
        x if x.size == 1 else pltpu.with_memory_space_constraint(x, pltpu.HBM) for x in ins
    )
    packed, flags, inverse, blocks, traces, lifts, held_rhs, now, response = call(
        first_kernel,
        [
            shape(2 * rows, LANES),
            shape(8 * -(-(2 + 2 * links) // 8), LANES),
            shape(2, block, block, dtype=BF16),
            shape(2, links, block, block, dtype=BF16),
            shape(faces, width, block, dtype=BF16),
            shape(faces * LANES, block, dtype=BF16),
            shape(2, block, columns),
            shape(2, block, columns),
            shape(3, block, LANES),
        ],
        ins,
        20 * unit,
        [
            pltpu.VMEM((2, block, block), BF16),
            *(pltpu.SMEM(x.shape, jnp.int32) for x in ins[:4]),
            pltpu.SemaphoreType.DMA((4,)),
            pltpu.SemaphoreType.DMA((3 + faces,)),
            pltpu.SemaphoreType.DMA((2 * links,)),
        ],
        [hbm] * len(ins),
    )
    table, square = pair(2, block, faces * LANES), pair(2, block, block)
    side_pair, line_pair = pair(2 * rows, 2 * LANES), pair(rows, 4 * LANES)
    store = {}

    def maps():
        return call(
            maps_kernel,
            [shape(2, block, columns), *table, *square, shape(2, rows, columns), *side_pair,
             shape(rows, LANES), *line_pair, *pair(block, LANES)],
            (flags, inverse, blocks, traces, lifts, held_rhs, now, response),
            40 * unit,
        )

    def more_maps():
        return call(
            more_maps_kernel,
            [*side_pair, *line_pair],
            (flags, traces, *store["d"], *store["e"], *store["last"]),
            16 * unit,
        )

    def parts_of(block, size, stride):
        sent = [exchange(block, "stream", size, stride, k) for k in reversed(range(1, size))]
        return [block] + sent

    def passage(key, size, stride):
        backward, level = key
        body = partial(passage_kernel, size, stride, backward)
        if level == len(levels) - 1 or (level == len(levels) - 2 and levels[-1][0] == 2):
            body, outs = partial(lambda f, *refs: f(*refs, None), body), []
        else:
            outs = [shape(2 * rows, LANES)]
        high, low, *whole = call(body, pair(rows, 2 * LANES) + outs, store["maps", key], 2 * unit)
        store["pass", key] = (high, low)
        store["whole", key] = whole

    def carried(total, backward, beside):
        befores, passes, done, stride_of_last = [], [], None, 0
        for level, (size, stride) in enumerate(levels):
            key = (backward, level)
            if level == len(levels) - 1 and size == 2:
                total, stride_of_last = exchange(total, "stream", size, stride, 1), stride
                break
            first = ("maps", key) not in store
            if first:
                first = "whole" if level else "packed"
                if level:
                    total = jnp.concatenate([total, *store["whole", (backward, level - 1)]], axis=0)
            parts = parts_of(total, size, stride)
            if level == 0:
                parts, done = lax.optimization_barrier((parts, beside()))
            held = shape(size, rows, columns)
            scratch = [pltpu.VMEM(held.shape, F32)]
            body = partial(fold_kernel, size, stride, backward, first)
            if first:
                outs = [trace, trace, *pair(size, rows, 2 * LANES)]
                total, before, *kept = call(body, outs, parts, unit, scratch)
                store["maps", key] = tuple(kept)
                passage(key, size, stride)
            elif ("suffix", key) in store:
                body = partial(total_kernel, size, stride, backward)
                total, held = call(body, [trace, held], (*parts, *store["suffix", key]), unit)
                body = partial(before_kernel, size, stride, backward)
                (before,) = call(body, [trace], (held, *store["maps", key]), unit)
            else:
                ins = (*parts, *store["maps", key])
                total, before = call(body, [trace, trace], ins, unit, scratch)
            befores.append(before)
            passes += store["pass", key]
        if not befores:
            befores = [jnp.zeros_like(total)]
            passes = [jnp.zeros((rows, 2 * LANES), BF16)] * 2
        return befores, passes, total, stride_of_last, done or beside()

    def suffixes(backward):
        out = {}
        for level, (size, _) in enumerate(levels):
            key = (backward, level)
            if ("maps", key) in store:
                outs = pair(rows, 2 * LANES * (size - 1))
                out["suffix", key] = call(
                    partial(suffix_kernel, size), outs, store["maps", key], unit
                )
        return out

    def send_maps(block):
        size, stride = levels[0]
        after = store["pass", (False, 0)]
        block, store["pass", (False, 0)] = lax.optimization_barrier((block, after))
        return parts_of(block, size, stride)

    def take_maps(parts):
        size, stride = levels[0]
        body = partial(unpack_kernel, size, stride, True)
        store["maps", (True, 0)] = tuple(call(body, pair(size, rows, 2 * LANES), parts, unit))
        passage((True, 0), size, stride)

    grouped = levels and not (len(levels) == 1 and levels[0][0] == 2)
    halves = [backward for _ in range(SWEEPS) for backward in (False, True)]
    for number, backward in enumerate(halves):
        final = number == len(halves) - 1
        if number == 0:
            befores, passes, arrived, stride, done = carried(packed, backward, maps)
            store["z"], store["d"], store["e"], side = done[0], done[1:3], done[3:5], done[5]
            store["side", False], store["line", True] = done[6:8], done[9:11]
            store["last"] = done[11:13]
            line = now[0]
            if grouped:
                sent = send_maps(done[8])
        else:
            (outflow,) = call(
                partial(outflow_kernel, involution),
                [trace],
                (base, *store["line", backward], first, second),
                unit,
            )
            body = partial(field_kernel, backward, involution)
            outs = [field, field] if final else [field, shape(2, rows, columns)]
            ins = (flags, first, second, start, left, *store["d"], *store["e"], traces)
            cut = len(ins) + (2 if final else 1)
            body = partial(lambda f, n, *refs: f(*refs[:n], None, *refs[n:]), body, cut)

            def beside():
                more = {}
                if number == 1:
                    out = more_maps()
                    more = {("side", True): out[:2], ("line", False): out[2:]}
                return call(body, outs, ins, 14 * unit), more

            if number == 1 and grouped:
                take_maps(sent)
            befores, passes, arrived, stride, done = carried(outflow, backward, beside)
            line, side = done[0]
            store.update(done[1])
        depth = len(befores)
        if final:
            wide = pair(2, block, 2 * LANES)
            body = partial(last_response_kernel, depth)
            out = call(body, wide + wide, (flags, *store["d"], *store["last"], *passes), 4 * unit)
            near, far = out[:2], out[2:]
            body = partial(base_kernel, depth)
            body = partial(lambda f, *refs: f(*refs[:-1], None, None, None, None, refs[-1]), body)
            (before,) = call(body, [trace], (*befores, *passes), unit)
            ins = (flags, line, side, *near, before)
            (base,) = call(last_base_kernel, [shape(2, block, columns)], ins, 2 * unit)
            body = partial(last_kernel, stride, backward)
            (x,) = call(body, [shape(2, block, columns)], (base, *far, arrived), 2 * unit)
            break
        if number < 2:
            store.update(suffixes(backward))
        if ("join", backward) not in store:
            ins = (*store["side", backward], *passes)
            body = partial(join_kernel, depth)
            store["join", backward] = call(body, pair(3 * rows, 2 * LANES), ins, unit)
        base, before = call(
            partial(base_kernel, depth),
            [shape(2, rows, columns), trace],
            (*befores, *passes, side, *store["side", backward]),
            unit,
        )
        inflow, first, second = call(
            partial(enter_kernel, stride, backward, involution),
            [trace] * 3,
            (base, before, *store["join", backward], arrived),
            unit,
        )
        first, second = side_exchange(first, second, involution)
        base, start, left = call(
            partial(prepare_kernel, backward),
            [trace, field, field],
            (flags, inflow, line, store["z"], *store["d"], *store["e"], traces),
            14 * unit,
        )
    return x[None, None]


def solution(mesh):
    placed = (
        P("stream", "span", None, None, None),
        P("stream", "span", None, None, None),
        P(),
        P(),
        P(),
        P("stream", "span", None),
        P("stream", "span"),
        P("stream", "span", None, None),
        P("stream", "span", None, None),
    )
    return jax.shard_map(
        local,
        mesh=mesh,
        in_specs=placed,
        out_specs=P("stream", "span", None, None, None),
        check_vma=False,
    )
```

```python
from functools import partial

import jax
import jax.numpy as jnp
from jax import lax
from jax.experimental import pallas as pl
from jax.experimental.pallas import tpu as pltpu
from jax.sharding import PartitionSpec as P

SWEEPS = 2
LANES = 128
F32 = jnp.float32
BF16 = jnp.bfloat16


def mm(a, b):
    return jnp.dot(a, b, preferred_element_type=F32)


def mm_t(a, b):
    return lax.dot_general(a, b, (((1,), (1,)), ((), ())), preferred_element_type=F32)


def two(x):
    high = x.astype(BF16)
    low = (x - high.astype(F32)).astype(BF16)
    return high, low


def exact_times(operator, x):
    n = x.shape[1]
    both = mm(operator, jnp.concatenate(two(x), axis=1))
    return both[:, :n] + both[:, n:]


def map_times(high, low, x):
    n = x.shape[1]
    x_high, x_low = two(x)
    both = mm(high, jnp.concatenate([x_high, x_low], axis=1))
    return both[:, :n] + both[:, n:] + mm(low, x_high)


def pad_rows(x):
    gap = jnp.zeros((LANES - x.shape[0], x.shape[1]), x.dtype)
    return jnp.concatenate([x, gap], axis=0)


def spread(x):
    width = x.shape[0] // 2
    return jnp.concatenate([pad_rows(x[:width]), pad_rows(x[width:])], axis=0)


def pick(flag, yes, no):
    return jnp.where(flag, yes, no)


def by_position(flag, x):
    width = x.shape[0] // 2
    return (
        pad_rows(pick(flag, x[:width], x[width:])),
        pad_rows(pick(flag, x[width:], x[:width])),
    )


def slot_map(flag, first, second, across, backward):
    none = jnp.zeros_like(across)
    if backward:
        lower, upper = pick(flag, none, across), pick(flag, across, none)
    else:
        lower, upper = pick(flag, across, none), pick(flag, none, across)
    return (
        jnp.concatenate([pick(flag, first, second), upper], axis=1),
        jnp.concatenate([lower, pick(flag, second, first)], axis=1),
    )


def pack_map(first, second, across, flag_value):
    width = first.shape[0]
    spare = LANES - width
    lane = lax.broadcasted_iota(jnp.int32, first.shape, 1)
    one = jnp.where(lane >= width, pltpu.roll(across, width, 1), first)
    rest = jnp.where(lane >= width, pltpu.roll(across, width - spare, 1), second)
    return one, jnp.where(lane >= 2 * width - spare, flag_value, rest)


def unpack_map(one, two_):
    width = one.shape[0]
    spare = LANES - width
    lane = lax.broadcasted_iota(jnp.int32, one.shape, 1)
    none = jnp.zeros_like(one)
    first = jnp.where(lane < width, one, none)
    second = jnp.where(lane < width, two_, none)
    across = jnp.where(lane < spare, pltpu.roll(one, LANES - width, 1), none)
    rest = pltpu.roll(two_, LANES - (width - spare), 1)
    across = jnp.where((lane >= spare) & (lane < width), rest, across)
    flag = jnp.broadcast_to(two_[0:1, LANES - 1 : LANES], (1, LANES)) > 0.5
    return first, second, across, flag


def call(body, outs, ins, flops=0, scratch=(), spaces=None):
    vmem = pl.BlockSpec(memory_space=pltpu.VMEM)
    moved = sum(x.size * x.dtype.itemsize for x in ins)
    moved += sum(o.size * o.dtype.itemsize for o in outs)
    return pl.pallas_call(
        body,
        out_shape=list(outs),
        in_specs=spaces or [vmem] * len(ins),
        out_specs=[vmem] * len(outs),
        scratch_shapes=list(scratch),
        compiler_params=pltpu.CompilerParams(vmem_limit_bytes=24 * 2**20),
        cost_estimate=pl.CostEstimate(flops=flops, bytes_accessed=moved, transcendentals=0),
    )(*ins)


def shape(*dims, dtype=F32):
    return jax.ShapeDtypeStruct(dims, dtype)


def pair(*dims):
    return [shape(*dims, dtype=BF16)] * 2


def face(ref, q, f, count=1):
    return ref[q, :, f * LANES : (f + count) * LANES]


def lift_times(high, low, q, f, x, count=1):
    return map_times(face(high, q, f, count), face(low, q, f, count), x)


def times_exact(x, operator):
    n = x.shape[0]
    both = mm(jnp.concatenate(two(x), axis=0), operator)
    return both[:n] + both[n:]


def first_kernel(order_in, count_in, links_in, types_in, rhs_in, inverse_in, table_in, traces_in,
                 lifts_in, packed, flags, inverse, blocks, trace, head, rhs, order, count, links,
                 types, small, large, own):
    faces = blocks.shape[0]
    width = trace.shape[0]
    columns = rhs.shape[2]
    scalars = [
        pltpu.make_async_copy(a, b, small.at[i])
        for i, (a, b) in enumerate(
            ((order_in, order), (types_in, types), (links_in, links), (count_in, count))
        )
    ]
    pairs = [
        (traces_in.at[1], trace),
        (inverse_in, inverse),
        (lifts_in.at[0], head.at[pl.ds(0, width), :]),
        (rhs_in, rhs),
    ]
    copies = [pltpu.make_async_copy(a, b, large.at[i]) for i, (a, b) in enumerate(pairs)]
    for c in scalars + copies:
        c.start()
    gap = head.at[pl.ds(width, LANES - width), :]
    gap[...] = jnp.zeros(gap.shape, BF16)
    flags[...] = jnp.zeros_like(flags)
    for c in scalars:
        c.wait()
    a, b = order[0], order[1]
    fetched = [
        pltpu.make_async_copy(table_in.at[types[b, m]], blocks.at[m], own.at[m])
        for m in range(faces)
    ]
    for c in fetched:
        c.start()
    alive = (count[0] > 1).astype(F32)
    flags[0:1, :] = jnp.full((1, LANES), (a == 0).astype(F32))
    flags[1:2, :] = jnp.full((1, LANES), alive)
    for q, s in enumerate((a, b)):
        for m in range(faces):
            row = 2 + q * faces + m
            flags[row : row + 1, :] = jnp.full((1, LANES), (links[s, m] < 2).astype(F32))
    for c in copies:
        c.wait()
    far = mm(trace[...], inverse[b]) * alive
    start = jnp.concatenate([exact_times(inverse[a], rhs[a]), mm_t(inverse[a], head[...])], axis=1)
    near = exact_times(trace[...], start)
    packed[pl.ds(pl.multiple_of(a * width, 8), width), :] = near[:, :columns]
    far_high, far_low = two(far)
    lifted = mm_t(far_high, head[...]) + mm_t(far_low, head[...])
    shown = map_times(far_high, far_low, rhs[b])
    met = None
    for m in range(faces):
        fetched[m].wait()
        product = times_exact(far, blocks[m]) * (links[b, m] < 2).astype(F32)
        met = product if met is None else met + product
    met_high, met_low = two(met)
    met = map_times(met_high, met_low, start)
    packed[pl.ds(pl.multiple_of(b * width, 8), width), :] = shown - met[:, :columns]
    one, rest = pack_map(-near[:, columns:], -lifted, met[:, columns:], flags[0:1, :])
    packed[2 * width : 3 * width, :] = one
    packed[3 * width : 4 * width, :] = rest


def side_traces(out, traces, flag, first, second):
    width = traces.shape[1]
    n = first.shape[1]
    for f in (2, 3):
        shown = exact_times(traces[f], jnp.concatenate([first, second], axis=1))
        out[f - 2, :width, :] = pick(flag, shown[:, :n], shown[:, n:])
        out[f - 2, width:, :] = pick(flag, shown[:, n:], shown[:, :n])


def store_side_map(high, low, traces, flag, first, second, across, backward):
    width = traces.shape[1]
    for f in (2, 3):
        shown = exact_times(traces[f], jnp.concatenate([first, second, across], axis=1))
        rows = slot_map(
            flag, -shown[:, :LANES], -shown[:, LANES : 2 * LANES], shown[:, 2 * LANES :], backward
        )
        for s in (0, 1):
            place = ((f - 2) * 2 + s) * width
            high[place : place + width, :], low[place : place + width, :] = two(rows[s])


def store_line_map(high, low, flag, first, second, across, backward):
    width = first.shape[0]
    for f in (0, 1):
        lanes = slice(f * LANES, (f + 1) * LANES)
        rows = slot_map(flag, -first[:, lanes], -second[:, lanes], across[:, lanes], backward)
        for s in (0, 1):
            place, held = slice(s * width, (s + 1) * width), slice(2 * f * LANES, 2 * (f + 1) * LANES)
            high[place, held], low[place, held] = two(rows[s])


def maps_kernel(order_in, types_in, rhs_in, inverse_in, table_in, traces_in, lifts_in, flags,
                traces, z, d_high, d_low, e_high, e_low, side, side_high, side_low, back_map,
                q_high, q_low, last_high, last_low,
                inverse, rhs, lifts, blocks, order, types, small, large):
    width = traces.shape[1]
    links = blocks.shape[1]
    pairs = [(inverse_in, inverse), (rhs_in, rhs), (traces_in, traces)]
    for f in range(lifts_in.shape[0]):
        pairs.append((lifts_in.at[f], lifts.at[pl.ds(f * LANES, width), :]))
    scalars = [
        pltpu.make_async_copy(order_in, order, small.at[0]),
        pltpu.make_async_copy(types_in, types, small.at[1]),
    ]
    copies = [pltpu.make_async_copy(a, b, large.at[i]) for i, (a, b) in enumerate(pairs)]
    for c in scalars + copies:
        c.start()
    for f in range(lifts_in.shape[0]):
        gap = lifts.at[pl.ds(f * LANES + width, LANES - width), :]
        gap[...] = jnp.zeros(gap.shape, BF16)
    for c in scalars:
        c.wait()
    own = [
        pltpu.make_async_copy(
            table_in.at[types[order[q], m]], blocks.at[q, m], large.at[len(pairs) + q * links + m]
        )
        for q in (0, 1)
        for m in range(links)
    ]
    for c in own:
        c.start()
    for c in copies + own:
        c.wait()
    flag = flags[0:1, :] > 0.5
    for q in (0, 1):
        s = order[q]
        scale = flags[1:2, 0:1] if q else 1.0
        z[q] = exact_times(inverse[s], rhs[s]) * scale
        d_high[q], d_low[q] = two(mm_t(inverse[s], lifts[...]) * scale)
        total = None
        for m in range(links):
            row = 2 + q * links + m
            block = blocks[q, m].astype(F32) * flags[row : row + 1, 0:1]
            total = block if total is None else total + block
        high, low = two(total)
        e_high[q], e_low[q] = two((mm(inverse[s], high) + mm(inverse[s], low)) * scale)

    def lift_of(q):
        return face(d_high, q, 0).astype(F32) + face(d_low, q, 0).astype(F32)

    n = z.shape[2]
    met = jnp.concatenate([z[0], lift_of(0)], axis=1)
    met = map_times(e_high[1], e_low[1], met)
    side_traces(side, traces, flag, z[0], z[1] - met[:, :n])
    store_side_map(
        side_high, side_low, traces, flag, lift_of(0), lift_of(1), met[:, n:], False
    )
    faces = lifts.shape[0] // LANES - 1
    high, low = face(d_high, 1, 1, faces), face(d_low, 1, 1, faces)
    both = mm(e_high[0], jnp.concatenate([high, low], axis=1))
    n = faces * LANES
    across = both[:, :n] + both[:, n:] + mm(e_low[0], high)
    last_high[...], last_low[...] = two(across[:, :LANES])
    shown = []
    for q in (0, 1):
        shown.append(
            mm(traces[0], face(d_high, q, 1, faces)) + mm(traces[0], face(d_low, q, 1, faces))
        )
    shown.append(exact_times(traces[0], across))
    one, rest = pack_map(
        -shown[0][:, :LANES], -shown[1][:, :LANES], shown[2][:, :LANES], flags[0:1, :]
    )
    back_map[:width, :] = one
    back_map[width:, :] = rest
    store_line_map(q_high, q_low, flag, *(s[:, LANES:] for s in shown), True)


def more_maps_kernel(flags, traces, d_high, d_low, e_high, e_low, last_high, last_low,
                     side_high, side_low, q_high, q_low):
    flag = flags[0:1, :] > 0.5

    def joined(q, f, count):
        return face(d_high, q, f, count).astype(F32) + face(d_low, q, f, count).astype(F32)

    across = last_high[...].astype(F32) + last_low[...].astype(F32)
    store_side_map(
        side_high, side_low, traces, flag, joined(0, 1, 1), joined(1, 1, 1), across, True
    )
    high, low = face(d_high, 0, 2, 2), face(d_low, 0, 2, 2)
    both = mm(e_high[1], jnp.concatenate([high, low], axis=1))
    n = 2 * LANES
    across = both[:, :n] + both[:, n:] + mm(e_low[1], high)
    shown = exact_times(
        traces[1], jnp.concatenate([joined(0, 2, 2), joined(1, 2, 2), across], axis=1)
    )
    store_line_map(
        q_high, q_low, flag, shown[:, :n], shown[:, n : 2 * n], shown[:, 2 * n :], False
    )


def prepare_kernel(backward, flags, inflow, line, z, d_high, d_low, e_high, e_low, traces,
                   outflow, field, other):
    p0, p1 = (1, 0) if backward else (0, 1)
    f = 1 if backward else 0
    flag = flags[0:1, :] > 0.5
    entered = by_position(flag, inflow[...])
    width = traces.shape[1]
    lifted = lift_times(d_high, d_low, p0, f, entered[p0])
    y = line[...] - lifted
    start = z[p1] - lift_times(d_high, d_low, p1, f, entered[p1])
    start = start - map_times(e_high[p1], e_low[p1], y)
    field[...] = start
    left = z[p0] - lifted
    other[...] = left
    end = left - map_times(e_high[p0], e_low[p0], start)
    fields = (start, end) if p1 == 0 else (end, start)
    n = start.shape[1]
    shown = exact_times(traces[1 if backward else 0], jnp.concatenate(fields, axis=1))
    outflow[:width, :] = pick(flag, shown[:, :n], shown[:, n:])
    outflow[width:, :] = pick(flag, shown[:, n:], shown[:, :n])


def sides(involution, first, second):
    if not involution:
        return first[...], second[...]
    odd = lax.rem(lax.axis_index("span"), 2) == 1
    return pick(odd, first[...], second[...]), pick(odd, second[...], first[...])


def outflow_kernel(involution, base, q_high, q_low, first, second, outflow):
    arrived = jnp.concatenate([spread(v) for v in sides(involution, first, second)], axis=0)
    outflow[...] = base[...] + map_times(q_high[...], q_low[...], arrived)


def field_kernel(backward, involution, flags, first, second, start, left, d_high, d_low, e_high,
                 e_low, traces, line, second_line, side):
    p0, p1 = (1, 0) if backward else (0, 1)
    flag = flags[0:1, :] > 0.5
    arrived = [by_position(flag, v) for v in sides(involution, first, second)]

    def lifted(q):
        both = jnp.concatenate([v[q] for v in arrived], axis=0)
        return lift_times(d_high, d_low, q, 2, both, 2)

    y0 = start[...] - lifted(p0)
    line[...] = y0
    y1 = left[...] - lifted(p1) - map_times(e_high[p1], e_low[p1], y0)
    if second_line is not None:
        second_line[...] = y1
    if side is not None:
        fields = (y1, y0) if backward else (y0, y1)
        side_traces(side, traces, flag, *fields)


def last_response_kernel(depth, flags, d_high, d_low, last_high, last_low, *refs):
    passes, (high, low, far_high, far_low) = refs[:-4], refs[-4:]
    flag = flags[0:1, :] > 0.5
    none = jnp.zeros((d_high.shape[1], LANES), F32)

    def joined(h, l):
        return h.astype(F32) + l.astype(F32)

    own = -joined(face(d_high, 0, 1), face(d_low, 0, 1))
    other = -joined(face(d_high, 1, 1), face(d_low, 1, 1))
    across = joined(last_high[...], last_low[...])
    rows = slot_map(flag, own, other, across, True)
    for s in (0, 1):
        high[s], low[s] = two(rows[s])
        far_high[s], far_low[s] = two(through(high[s], low[s], depth, passes))


def last_base_kernel(flags, line, second_line, high, low, inflow, out):
    flag = flags[0:1, :] > 0.5
    entered = spread(inflow[...])
    out[0] = pick(flag, second_line[...], line[...]) + map_times(high[0], low[0], entered)
    out[1] = pick(flag, line[...], second_line[...]) + map_times(high[1], low[1], entered)


def last_kernel(stride, backward, base, high, low, arrived, out):
    entered = spread(last_arrived(stride, backward, arrived))
    for s in (0, 1):
        out[s] = base[s] + map_times(high[s], low[s], entered)


def digit_of(size, stride):
    return lax.rem(lax.div(lax.axis_index("stream"), stride), size)


def place_of(size, stride, backward):
    digit = digit_of(size, stride)
    return size - 1 - digit if backward else digit


def source_place(size, stride, backward, i):
    digit, k = digit_of(size, stride), (size - i) % size
    m = digit ^ k if size & (size - 1) == 0 else lax.rem(digit - k + size, size)
    return size - 1 - m if backward else m


def store_packed(high, low, m, packed, backward):
    width = packed.shape[0] // 2
    a, b, c, flag = unpack_map(packed[:width], packed[width:])
    for s, row in enumerate(slot_map(flag, a, b, c, backward)):
        high[m, s * width : (s + 1) * width], low[m, s * width : (s + 1) * width] = two(row)


def in_turn(size, place, values, high, low):
    state = values[0]
    below = jnp.zeros_like(state)
    for m in range(1, size):
        below = jnp.where(place == m, state, below)
        if m < size:
            state = values[m] + map_times(high[m], low[m], spread(state))
    return state, below


def fold_kernel(size, stride, backward, first, *refs):
    parts, refs = refs[:size], refs[size:]
    if first:
        total, before, high, low, held = refs
    else:
        high, low, total, before, held = refs
    rows = total.shape[0]
    for i, part in enumerate(parts):
        m = source_place(size, stride, backward, i)
        held[m] = part[:rows, :]
        if first == "packed":
            store_packed(high, low, m, part[rows:, :], backward)
        elif first:
            for f in (0, 1):
                a, b = two(part[rows * (1 + f) : rows * (2 + f), :])
                high[m, :, f * LANES : (f + 1) * LANES] = a
                low[m, :, f * LANES : (f + 1) * LANES] = b
    place = place_of(size, stride, backward)
    total[...], before[...] = in_turn(size, place, held, high, low)


def unpack_kernel(size, stride, backward, *refs):
    parts, (high, low) = refs[:size], refs[size:]
    for i, part in enumerate(parts):
        store_packed(high, low, source_place(size, stride, backward, i), part[...], backward)


def total_kernel(size, stride, backward, *refs):
    parts, (high, low, total, held) = refs[:size], refs[size:]
    for i, part in enumerate(parts):
        held[source_place(size, stride, backward, i)] = part[...]
    below = jnp.concatenate([spread(held[m]) for m in range(size - 1)], axis=0)
    total[...] = held[size - 1] + map_times(high[...], low[...], below)


def before_kernel(size, stride, backward, held, high, low, before):
    place = place_of(size, stride, backward)
    _, before[...] = in_turn(size, place, held, high, low)


def suffix_kernel(size, high, low, out_high, out_low):
    state_high, state_low = high[size - 1], low[size - 1]
    for m in reversed(range(size - 1)):
        lanes = slice(2 * LANES * m, 2 * LANES * (m + 1))
        out_high[:, lanes], out_low[:, lanes] = state_high, state_low
        if m:
            inner = high[m].astype(F32) + low[m].astype(F32)
            state_high, state_low = two(map_times(state_high, state_low, spread(inner)))


def passage_kernel(size, stride, backward, high, low, pass_high, pass_low, whole):
    rows = high.shape[1]
    width = rows // 2
    place = place_of(size, stride, backward)
    row = lax.broadcasted_iota(jnp.int32, (rows, 2 * LANES), 0)
    lane = lax.broadcasted_iota(jnp.int32, (rows, 2 * LANES), 1)
    moved = jnp.where(row < width, row, row - width + LANES)
    state = jnp.where(moved == lane, 1.0, 0.0)
    kept = state
    for m in range(size):
        kept = jnp.where(place == m, state, kept)
        if m < size - 1 or whole is not None:
            if m:
                state = map_times(high[m], low[m], spread(state))
            else:
                state = high[0].astype(F32) + low[0].astype(F32)
    pass_high[...], pass_low[...] = two(kept)
    if whole is not None:
        whole[:rows, :] = state[:, :LANES]
        whole[rows:, :] = state[:, LANES:]


def through(high, low, depth, passes):
    state = None
    for level in range(depth):
        if state is not None:
            high, low = two(state)
        inner = passes[2 * level][...].astype(F32) + passes[2 * level + 1][...].astype(F32)
        state = map_times(high, low, spread(inner))
    return high.astype(F32) + low.astype(F32) if state is None else state


def join_kernel(depth, side_high, side_low, *refs):
    passes, (high, low) = refs[:-2], refs[-2:]
    rows = side_high.shape[0]
    high[:rows], low[:rows] = two(through(side_high[...], side_low[...], depth, passes))
    if depth == 1:
        high[rows:], low[rows:] = passes[0][...], passes[1][...]
    else:
        high[rows:], low[rows:] = two(through(passes[0][...], passes[1][...], depth - 1, passes[2:]))


def base_kernel(depth, *refs):
    befores, refs = refs[:depth], refs[depth:]
    passes, refs = refs[: 2 * depth], refs[2 * depth :]
    side, high, low, base, inflow = refs
    state = befores[depth - 1][...]
    for level in reversed(range(depth - 1)):
        inner = map_times(passes[2 * level][...], passes[2 * level + 1][...], spread(state))
        state = befores[level][...] + inner
    inflow[...] = state
    if base is not None:
        both = map_times(high[...], low[...], spread(state))
        rows = state.shape[0]
        base[0] = side[0] + both[:rows]
        base[1] = side[1] + both[rows:]


def last_arrived(stride, backward, arrived):
    if not stride:
        return jnp.zeros(arrived.shape, F32)
    upper = digit_of(2, stride) == (0 if backward else 1)
    return jnp.where(upper, arrived[...], 0.0)


def enter_kernel(stride, backward, involution, base, before, high, low, arrived,
                 inflow, first, second):
    rows = inflow.shape[0]
    entered = spread(last_arrived(stride, backward, arrived))
    added = map_times(high[...], low[...], entered)
    inflow[...] = before[...] + added[2 * rows :]
    lower_face = base[0] + added[:rows]
    upper_face = base[1] + added[rows : 2 * rows]
    if involution:
        odd = lax.rem(lax.axis_index("span"), 2) == 1
        first[...] = pick(odd, lower_face, upper_face)
        second[...] = pick(odd, upper_face, lower_face)
    else:
        first[...] = upper_face
        second[...] = lower_face


def levels_of(count):
    sizes, left = [], count
    for factor in (4, 2):
        while left % factor == 0:
            sizes.append(factor)
            left //= factor
    factor = 3
    while left > 1:
        while left % factor == 0:
            sizes.insert(0, factor)
            left //= factor
        factor += 2
    strides, stride = [], 1
    for size in sizes:
        strides.append(stride)
        stride *= size
    return list(zip(sizes, strides))


def exchange(block, axis, size, stride, k):
    pairs = []
    for i in range(lax.axis_size(axis)):
        digit = (i // stride) % size
        target = digit ^ k if size & (size - 1) == 0 else (digit + k) % size
        pairs.append((i, i + (target - digit) * stride))
    return lax.ppermute(block, axis, pairs)


def side_exchange(first, second, involution):
    n = lax.axis_size("span")
    if involution:
        pairs = [(j, j ^ 1) for j in range(n)]
        across = [(j, (j + 1) % n if j % 2 else (j - 1) % n) for j in range(n)]
        second = lax.ppermute(second, "span", across)
        first = lax.ppermute(first, "span", pairs)
        return first, second
    return (
        lax.ppermute(first, "span", [(j, (j + 1) % n) for j in range(n)]),
        lax.ppermute(second, "span", [(j, (j - 1) % n) for j in range(n)]),
    )


def local(rhs, inv_blocks, coupling, trace_ops, lift_ops, order, counts, neighbours, face_ids):
    source, inverse_in = rhs[0, 0], inv_blocks[0, 0]
    slots, block, columns = source.shape
    faces, width = trace_ops.shape[:2]
    links = neighbours.shape[-1]
    rows = 2 * width
    if slots != 2 or columns % LANES or 3 * width >= 2 * LANES:
        raise ValueError("unsupported sizes")
    levels = levels_of(lax.axis_size("stream"))
    span = lax.axis_size("span")
    involution = span % 2 == 0 and span > 2

    field, trace = shape(block, columns), shape(rows, columns)
    unit = 2 * block * block * LANES
    hbm = pl.BlockSpec(memory_space=pl.ANY)
    given = (order[0, 0], counts[0], neighbours[0, 0], face_ids[0, 0], source, inverse_in, coupling,
           trace_ops, jnp.swapaxes(lift_ops, 1, 2))
    inputs = tuple(
        x if x.size == 1 else pltpu.with_memory_space_constraint(x, pltpu.HBM) for x in given
    )
    packed, flags = call(
        first_kernel,
        [shape(2 * rows, LANES), shape(8 * -(-(2 + 2 * links) // 8), LANES)],
        inputs,
        20 * unit,
        [
            pltpu.VMEM((2, block, block), BF16),
            pltpu.VMEM((links, block, block), BF16),
            pltpu.VMEM((width, block), BF16),
            pltpu.VMEM((LANES, block), BF16),
            pltpu.VMEM((2, block, columns), F32),
            *(pltpu.SMEM(x.shape, jnp.int32) for x in inputs[:4]),
            pltpu.SemaphoreType.DMA((4,)),
            pltpu.SemaphoreType.DMA((4,)),
            pltpu.SemaphoreType.DMA((links,)),
        ],
        [hbm] * len(inputs),
    )
    table, square = pair(2, block, faces * LANES), pair(2, block, block)
    side_pair, line_pair = pair(2 * rows, 2 * LANES), pair(rows, 4 * LANES)
    store = {}

    def maps():
        held = (inputs[0], *inputs[3:])
        return call(
            maps_kernel,
            [shape(*trace_ops.shape, dtype=BF16), shape(2, block, columns), *table, *square,
             shape(2, rows, columns), *side_pair, shape(rows, LANES), *line_pair,
             *pair(block, LANES)],
            (*held, flags),
            50 * unit,
            [
                pltpu.VMEM((2, block, block), BF16),
                pltpu.VMEM((2, block, columns), F32),
                pltpu.VMEM((faces * LANES, block), BF16),
                pltpu.VMEM((2, links, block, block), BF16),
                *(pltpu.SMEM(x.shape, jnp.int32) for x in held[:2]),
                pltpu.SemaphoreType.DMA((2,)),
                pltpu.SemaphoreType.DMA((3 + faces + 2 * links,)),
            ],
            [hbm] * len(held) + [pl.BlockSpec(memory_space=pltpu.VMEM)],
        )

    def more_maps():
        return call(
            more_maps_kernel,
            [*side_pair, *line_pair],
            (flags, traces, *store["d"], *store["e"], *store["last"]),
            16 * unit,
        )

    def parts_of(block, size, stride):
        sent = [exchange(block, "stream", size, stride, k) for k in reversed(range(1, size))]
        return [block] + sent

    def passage(key, size, stride):
        backward, level = key
        body = partial(passage_kernel, size, stride, backward)
        if level == len(levels) - 1 or (level == len(levels) - 2 and levels[-1][0] == 2):
            body, outs = partial(lambda f, *refs: f(*refs, None), body), []
        else:
            outs = [shape(2 * rows, LANES)]
        high, low, *whole = call(body, pair(rows, 2 * LANES) + outs, store["maps", key], 2 * unit)
        store["pass", key] = (high, low)
        store["whole", key] = whole

    def carried(total, backward, beside):
        befores, passes, done, stride_of_last = [], [], None, 0
        for level, (size, stride) in enumerate(levels):
            key = (backward, level)
            if level == len(levels) - 1 and size == 2:
                total, stride_of_last = exchange(total, "stream", size, stride, 1), stride
                break
            first = ("maps", key) not in store
            if first:
                first = "whole" if level else "packed"
                if level:
                    total = jnp.concatenate([total, *store["whole", (backward, level - 1)]], axis=0)
            parts = parts_of(total, size, stride)
            if level == 0:
                parts, done = lax.optimization_barrier((parts, beside()))
            held = shape(size, rows, columns)
            scratch = [pltpu.VMEM(held.shape, F32)]
            body = partial(fold_kernel, size, stride, backward, first)
            if first:
                outs = [trace, trace, *pair(size, rows, 2 * LANES)]
                total, before, *kept = call(body, outs, parts, unit, scratch)
                store["maps", key] = tuple(kept)
                passage(key, size, stride)
            elif ("suffix", key) in store:
                body = partial(total_kernel, size, stride, backward)
                total, held = call(body, [trace, held], (*parts, *store["suffix", key]), unit)
                body = partial(before_kernel, size, stride, backward)
                (before,) = call(body, [trace], (held, *store["maps", key]), unit)
            else:
                ins = (*parts, *store["maps", key])
                total, before = call(body, [trace, trace], ins, unit, scratch)
            befores.append(before)
            passes += store["pass", key]
        if not befores:
            befores = [jnp.zeros_like(total)]
            passes = [jnp.zeros((rows, 2 * LANES), BF16)] * 2
        return befores, passes, total, stride_of_last, done or beside()

    def suffixes(backward):
        out = {}
        for level, (size, _) in enumerate(levels):
            key = (backward, level)
            if ("maps", key) in store:
                outs = pair(rows, 2 * LANES * (size - 1))
                out["suffix", key] = call(
                    partial(suffix_kernel, size), outs, store["maps", key], unit
                )
        return out

    def send_maps(block):
        size, stride = levels[0]
        after = store["pass", (False, 0)]
        block, store["pass", (False, 0)] = lax.optimization_barrier((block, after))
        return parts_of(block, size, stride)

    def take_maps(parts):
        size, stride = levels[0]
        body = partial(unpack_kernel, size, stride, True)
        store["maps", (True, 0)] = tuple(call(body, pair(size, rows, 2 * LANES), parts, unit))
        passage((True, 0), size, stride)

    grouped = levels and not (len(levels) == 1 and levels[0][0] == 2)
    halves = [backward for _ in range(SWEEPS) for backward in (False, True)]
    for number, backward in enumerate(halves):
        final = number == len(halves) - 1
        if number == 0:
            befores, passes, arrived, stride, done = carried(packed, backward, maps)
            traces, *done = done
            store["z"], store["d"], store["e"], side = done[0], done[1:3], done[3:5], done[5]
            store["side", False], store["line", True] = done[6:8], done[9:11]
            store["last"] = done[11:13]
            line = store["z"][0]
            if grouped:
                sent = send_maps(done[8])
        else:
            (outflow,) = call(
                partial(outflow_kernel, involution),
                [trace],
                (base, *store["line", backward], first, second),
                unit,
            )
            body = partial(field_kernel, backward, involution)
            outs = [field, field] if final else [field, shape(2, rows, columns)]
            ins = (flags, first, second, start, left, *store["d"], *store["e"], traces)
            cut = len(ins) + (2 if final else 1)
            body = partial(lambda f, n, *refs: f(*refs[:n], None, *refs[n:]), body, cut)

            def beside():
                more = {}
                if number == 1:
                    out = more_maps()
                    more = {("side", True): out[:2], ("line", False): out[2:]}
                return call(body, outs, ins, 14 * unit), more

            if number == 1 and grouped:
                take_maps(sent)
                store.update(suffixes(True))
            befores, passes, arrived, stride, done = carried(outflow, backward, beside)
            line, side = done[0]
            store.update(done[1])
        depth = len(befores)
        if final:
            wide = pair(2, block, 2 * LANES)
            body = partial(last_response_kernel, depth)
            out = call(body, wide + wide, (flags, *store["d"], *store["last"], *passes), 4 * unit)
            near, far = out[:2], out[2:]
            body = partial(base_kernel, depth)
            body = partial(lambda f, *refs: f(*refs[:-1], None, None, None, None, refs[-1]), body)
            (before,) = call(body, [trace], (*befores, *passes), unit)
            ins = (flags, line, side, *near, before)
            (base,) = call(last_base_kernel, [shape(2, block, columns)], ins, 2 * unit)
            body = partial(last_kernel, stride, backward)
            (x,) = call(body, [shape(2, block, columns)], (base, *far, arrived), 2 * unit)
            break
        if number == 0:
            store.update(suffixes(False))
        if ("join", backward) not in store:
            ins = (*store["side", backward], *passes)
            body = partial(join_kernel, depth)
            store["join", backward] = call(body, pair(3 * rows, 2 * LANES), ins, unit)
        base, before = call(
            partial(base_kernel, depth),
            [shape(2, rows, columns), trace],
            (*befores, *passes, side, *store["side", backward]),
            unit,
        )
        inflow, first, second = call(
            partial(enter_kernel, stride, backward, involution),
            [trace] * 3,
            (base, before, *store["join", backward], arrived),
            unit,
        )
        first, second = side_exchange(first, second, involution)
        base, start, left = call(
            partial(prepare_kernel, backward),
            [trace, field, field],
            (flags, inflow, line, store["z"], *store["d"], *store["e"], traces),
            14 * unit,
        )
    return x[None, None]


def solution(mesh):
    placed = (
        P("stream", "span", None, None, None),
        P("stream", "span", None, None, None),
        P(),
        P(),
        P(),
        P("stream", "span", None),
        P("stream", "span"),
        P("stream", "span", None, None),
        P("stream", "span", None, None),
    )
    return jax.shard_map(
        local,
        mesh=mesh,
        in_specs=placed,
        out_specs=P("stream", "span", None, None, None),
        check_vma=False,
    )
```

```python
from functools import partial

import jax
import jax.numpy as jnp
from jax import lax
from jax.experimental import pallas as pl
from jax.experimental.pallas import tpu as pltpu
from jax.sharding import PartitionSpec as P

SWEEPS = 2
LANES = 128
F32 = jnp.float32
BF16 = jnp.bfloat16


def mm(a, b):
    return jnp.dot(a, b, preferred_element_type=F32)


def mm_t(a, b):
    return lax.dot_general(a, b, (((1,), (1,)), ((), ())), preferred_element_type=F32)


def two(x):
    high = x.astype(BF16)
    low = (x - high.astype(F32)).astype(BF16)
    return high, low


def exact_times(operator, x):
    n = x.shape[1]
    both = mm(operator, jnp.concatenate(two(x), axis=1))
    return both[:, :n] + both[:, n:]


def map_times(high, low, x):
    n = x.shape[1]
    x_high, x_low = two(x)
    both = mm(high, jnp.concatenate([x_high, x_low], axis=1))
    return both[:, :n] + both[:, n:] + mm(low, x_high)


def pad_rows(x):
    gap = jnp.zeros((LANES - x.shape[0], x.shape[1]), x.dtype)
    return jnp.concatenate([x, gap], axis=0)


def spread(x):
    width = x.shape[0] // 2
    return jnp.concatenate([pad_rows(x[:width]), pad_rows(x[width:])], axis=0)


def pick(flag, yes, no):
    return jnp.where(flag, yes, no)


def by_position(flag, x):
    width = x.shape[0] // 2
    return (
        pad_rows(pick(flag, x[:width], x[width:])),
        pad_rows(pick(flag, x[width:], x[:width])),
    )


def slot_map(flag, first, second, across, backward):
    none = jnp.zeros_like(across)
    if backward:
        lower, upper = pick(flag, none, across), pick(flag, across, none)
    else:
        lower, upper = pick(flag, across, none), pick(flag, none, across)
    return (
        jnp.concatenate([pick(flag, first, second), upper], axis=1),
        jnp.concatenate([lower, pick(flag, second, first)], axis=1),
    )


def pack_map(first, second, across, flag_value):
    width = first.shape[0]
    spare = LANES - width
    lane = lax.broadcasted_iota(jnp.int32, first.shape, 1)
    one = jnp.where(lane >= width, pltpu.roll(across, width, 1), first)
    rest = jnp.where(lane >= width, pltpu.roll(across, width - spare, 1), second)
    return one, jnp.where(lane >= 2 * width - spare, flag_value, rest)


def unpack_map(one, two_):
    width = one.shape[0]
    spare = LANES - width
    lane = lax.broadcasted_iota(jnp.int32, one.shape, 1)
    none = jnp.zeros_like(one)
    first = jnp.where(lane < width, one, none)
    second = jnp.where(lane < width, two_, none)
    across = jnp.where(lane < spare, pltpu.roll(one, LANES - width, 1), none)
    rest = pltpu.roll(two_, LANES - (width - spare), 1)
    across = jnp.where((lane >= spare) & (lane < width), rest, across)
    flag = jnp.broadcast_to(two_[0:1, LANES - 1 : LANES], (1, LANES)) > 0.5
    return first, second, across, flag


def call(body, outs, ins, flops=0, scratch=(), spaces=None):
    vmem = pl.BlockSpec(memory_space=pltpu.VMEM)
    moved = sum(x.size * x.dtype.itemsize for x in ins)
    moved += sum(o.size * o.dtype.itemsize for o in outs)
    return pl.pallas_call(
        body,
        out_shape=list(outs),
        in_specs=spaces or [vmem] * len(ins),
        out_specs=[vmem] * len(outs),
        scratch_shapes=list(scratch),
        compiler_params=pltpu.CompilerParams(vmem_limit_bytes=24 * 2**20),
        cost_estimate=pl.CostEstimate(flops=flops, bytes_accessed=moved, transcendentals=0),
    )(*ins)


def shape(*dims, dtype=F32):
    return jax.ShapeDtypeStruct(dims, dtype)


def pair(*dims):
    return [shape(*dims, dtype=BF16)] * 2


def face(ref, q, f, count=1):
    return ref[q, :, f * LANES : (f + count) * LANES]


def lift_times(high, low, q, f, x, count=1):
    return map_times(face(high, q, f, count), face(low, q, f, count), x)


def times_exact(x, operator):
    n = x.shape[0]
    both = mm(jnp.concatenate(two(x), axis=0), operator)
    return both[:n] + both[n:]


def first_kernel(order_in, count_in, links_in, types_in, rhs_in, inverse_in, table_in, traces_in,
                 lifts_in, packed, flags, inverse, blocks, trace, head, rhs, order, count, links,
                 types, small, large, own):
    faces = blocks.shape[0]
    width = trace.shape[0]
    columns = rhs.shape[2]
    scalars = [
        pltpu.make_async_copy(a, b, small.at[i])
        for i, (a, b) in enumerate(
            ((order_in, order), (types_in, types), (links_in, links), (count_in, count))
        )
    ]
    pairs = [
        (traces_in.at[1], trace),
        (inverse_in, inverse),
        (lifts_in.at[0], head.at[pl.ds(0, width), :]),
        (rhs_in, rhs),
    ]
    copies = [pltpu.make_async_copy(a, b, large.at[i]) for i, (a, b) in enumerate(pairs)]
    for c in scalars + copies:
        c.start()
    gap = head.at[pl.ds(width, LANES - width), :]
    gap[...] = jnp.zeros(gap.shape, BF16)
    flags[...] = jnp.zeros_like(flags)
    for c in scalars:
        c.wait()
    a, b = order[0], order[1]
    fetched = [
        pltpu.make_async_copy(table_in.at[types[b, m]], blocks.at[m], own.at[m])
        for m in range(faces)
    ]
    for c in fetched:
        c.start()
    alive = (count[0] > 1).astype(F32)
    flags[0:1, :] = jnp.full((1, LANES), (a == 0).astype(F32))
    flags[1:2, :] = jnp.full((1, LANES), alive)
    for q, s in enumerate((a, b)):
        for m in range(faces):
            row = 2 + q * faces + m
            flags[row : row + 1, :] = jnp.full((1, LANES), (links[s, m] < 2).astype(F32))
    for c in copies:
        c.wait()
    far = mm(trace[...], inverse[b]) * alive
    start = jnp.concatenate([exact_times(inverse[a], rhs[a]), mm_t(inverse[a], head[...])], axis=1)
    near = exact_times(trace[...], start)
    packed[pl.ds(pl.multiple_of(a * width, 8), width), :] = near[:, :columns]
    far_high, far_low = two(far)
    lifted = mm_t(far_high, head[...]) + mm_t(far_low, head[...])
    shown = map_times(far_high, far_low, rhs[b])
    met = None
    for m in range(faces):
        fetched[m].wait()
        product = times_exact(far, blocks[m]) * (links[b, m] < 2).astype(F32)
        met = product if met is None else met + product
    met_high, met_low = two(met)
    met = map_times(met_high, met_low, start)
    packed[pl.ds(pl.multiple_of(b * width, 8), width), :] = shown - met[:, :columns]
    one, rest = pack_map(-near[:, columns:], -lifted, met[:, columns:], flags[0:1, :])
    packed[2 * width : 3 * width, :] = one
    packed[3 * width : 4 * width, :] = rest


def side_traces(out, traces, flag, first, second):
    width = traces.shape[1]
    n = first.shape[1]
    for f in (2, 3):
        shown = exact_times(traces[f], jnp.concatenate([first, second], axis=1))
        out[f - 2, :width, :] = pick(flag, shown[:, :n], shown[:, n:])
        out[f - 2, width:, :] = pick(flag, shown[:, n:], shown[:, :n])


def store_side_map(high, low, traces, flag, first, second, across, backward):
    width = traces.shape[1]
    for f in (2, 3):
        shown = exact_times(traces[f], jnp.concatenate([first, second, across], axis=1))
        rows = slot_map(
            flag, -shown[:, :LANES], -shown[:, LANES : 2 * LANES], shown[:, 2 * LANES :], backward
        )
        for s in (0, 1):
            place = ((f - 2) * 2 + s) * width
            high[place : place + width, :], low[place : place + width, :] = two(rows[s])


def store_line_map(high, low, flag, first, second, across, backward):
    width = first.shape[0]
    for f in (0, 1):
        lanes = slice(f * LANES, (f + 1) * LANES)
        rows = slot_map(flag, -first[:, lanes], -second[:, lanes], across[:, lanes], backward)
        for s in (0, 1):
            place, held = slice(s * width, (s + 1) * width), slice(2 * f * LANES, 2 * (f + 1) * LANES)
            high[place, held], low[place, held] = two(rows[s])


def maps_kernel(order_in, types_in, rhs_in, inverse_in, table_in, traces_in, lifts_in, flags,
                traces, z, d_high, d_low, e_high, e_low, side, side_high, side_low, back_map,
                q_high, q_low, last_high, last_low,
                inverse, rhs, lifts, blocks, order, types, small, large):
    width = traces.shape[1]
    links = blocks.shape[1]
    pairs = [(inverse_in, inverse), (rhs_in, rhs), (traces_in, traces)]
    for f in range(lifts_in.shape[0]):
        pairs.append((lifts_in.at[f], lifts.at[pl.ds(f * LANES, width), :]))
    scalars = [
        pltpu.make_async_copy(order_in, order, small.at[0]),
        pltpu.make_async_copy(types_in, types, small.at[1]),
    ]
    copies = [pltpu.make_async_copy(a, b, large.at[i]) for i, (a, b) in enumerate(pairs)]
    for c in scalars + copies:
        c.start()
    for f in range(lifts_in.shape[0]):
        gap = lifts.at[pl.ds(f * LANES + width, LANES - width), :]
        gap[...] = jnp.zeros(gap.shape, BF16)
    for c in scalars:
        c.wait()
    own = [
        pltpu.make_async_copy(
            table_in.at[types[order[q], m]], blocks.at[q, m], large.at[len(pairs) + q * links + m]
        )
        for q in (0, 1)
        for m in range(links)
    ]
    for c in own:
        c.start()
    for c in copies + own:
        c.wait()
    flag = flags[0:1, :] > 0.5
    for q in (0, 1):
        s = order[q]
        scale = flags[1:2, 0:1] if q else 1.0
        z[q] = exact_times(inverse[s], rhs[s]) * scale
        d_high[q], d_low[q] = two(mm_t(inverse[s], lifts[...]) * scale)
        total = None
        for m in range(links):
            row = 2 + q * links + m
            block = blocks[q, m].astype(F32) * flags[row : row + 1, 0:1]
            total = block if total is None else total + block
        high, low = two(total)
        e_high[q], e_low[q] = two((mm(inverse[s], high) + mm(inverse[s], low)) * scale)

    def lift_of(q):
        return face(d_high, q, 0).astype(F32) + face(d_low, q, 0).astype(F32)

    n = z.shape[2]
    met = jnp.concatenate([z[0], lift_of(0)], axis=1)
    met = map_times(e_high[1], e_low[1], met)
    side_traces(side, traces, flag, z[0], z[1] - met[:, :n])
    store_side_map(
        side_high, side_low, traces, flag, lift_of(0), lift_of(1), met[:, n:], False
    )
    faces = lifts.shape[0] // LANES - 1
    high, low = face(d_high, 1, 1, faces), face(d_low, 1, 1, faces)
    both = mm(e_high[0], jnp.concatenate([high, low], axis=1))
    n = faces * LANES
    across = both[:, :n] + both[:, n:] + mm(e_low[0], high)
    last_high[...], last_low[...] = two(across[:, :LANES])
    shown = []
    for q in (0, 1):
        shown.append(
            mm(traces[0], face(d_high, q, 1, faces)) + mm(traces[0], face(d_low, q, 1, faces))
        )
    shown.append(exact_times(traces[0], across))
    one, rest = pack_map(
        -shown[0][:, :LANES], -shown[1][:, :LANES], shown[2][:, :LANES], flags[0:1, :]
    )
    back_map[:width, :] = one
    back_map[width:, :] = rest
    store_line_map(q_high, q_low, flag, *(s[:, LANES:] for s in shown), True)


def more_maps_kernel(flags, traces, d_high, d_low, e_high, e_low, last_high, last_low,
                     side_high, side_low, q_high, q_low):
    flag = flags[0:1, :] > 0.5

    def joined(q, f, count):
        return face(d_high, q, f, count).astype(F32) + face(d_low, q, f, count).astype(F32)

    across = last_high[...].astype(F32) + last_low[...].astype(F32)
    store_side_map(
        side_high, side_low, traces, flag, joined(0, 1, 1), joined(1, 1, 1), across, True
    )
    high, low = face(d_high, 0, 2, 2), face(d_low, 0, 2, 2)
    both = mm(e_high[1], jnp.concatenate([high, low], axis=1))
    n = 2 * LANES
    across = both[:, :n] + both[:, n:] + mm(e_low[1], high)
    shown = exact_times(
        traces[1], jnp.concatenate([joined(0, 2, 2), joined(1, 2, 2), across], axis=1)
    )
    store_line_map(
        q_high, q_low, flag, shown[:, :n], shown[:, n : 2 * n], shown[:, 2 * n :], False
    )


def prepare_kernel(backward, flags, inflow, line, z, d_high, d_low, e_high, e_low, traces,
                   outflow, field, other):
    p0, p1 = (1, 0) if backward else (0, 1)
    f = 1 if backward else 0
    flag = flags[0:1, :] > 0.5
    entered = by_position(flag, inflow[...])
    width = traces.shape[1]
    lifted = lift_times(d_high, d_low, p0, f, entered[p0])
    y = line[...] - lifted
    start = z[p1] - lift_times(d_high, d_low, p1, f, entered[p1])
    start = start - map_times(e_high[p1], e_low[p1], y)
    field[...] = start
    left = z[p0] - lifted
    other[...] = left
    end = left - map_times(e_high[p0], e_low[p0], start)
    fields = (start, end) if p1 == 0 else (end, start)
    n = start.shape[1]
    shown = exact_times(traces[1 if backward else 0], jnp.concatenate(fields, axis=1))
    outflow[:width, :] = pick(flag, shown[:, :n], shown[:, n:])
    outflow[width:, :] = pick(flag, shown[:, n:], shown[:, :n])


def sides(involution, first, second):
    if not involution:
        return first[...], second[...]
    odd = lax.rem(lax.axis_index("span"), 2) == 1
    return pick(odd, first[...], second[...]), pick(odd, second[...], first[...])


def outflow_kernel(involution, base, q_high, q_low, first, second, outflow):
    arrived = jnp.concatenate([spread(v) for v in sides(involution, first, second)], axis=0)
    outflow[...] = base[...] + map_times(q_high[...], q_low[...], arrived)


def field_kernel(backward, involution, flags, first, second, start, left, d_high, d_low, e_high,
                 e_low, traces, line, second_line, side):
    p0, p1 = (1, 0) if backward else (0, 1)
    flag = flags[0:1, :] > 0.5
    arrived = [by_position(flag, v) for v in sides(involution, first, second)]

    def lifted(q):
        both = jnp.concatenate([v[q] for v in arrived], axis=0)
        return lift_times(d_high, d_low, q, 2, both, 2)

    y0 = start[...] - lifted(p0)
    line[...] = y0
    y1 = left[...] - lifted(p1) - map_times(e_high[p1], e_low[p1], y0)
    if second_line is not None:
        second_line[...] = y1
    if side is not None:
        fields = (y1, y0) if backward else (y0, y1)
        side_traces(side, traces, flag, *fields)


def last_response_kernel(depth, flags, d_high, d_low, last_high, last_low, *refs):
    passes, (high, low, far_high, far_low) = refs[:-4], refs[-4:]
    flag = flags[0:1, :] > 0.5
    none = jnp.zeros((d_high.shape[1], LANES), F32)

    def joined(h, l):
        return h.astype(F32) + l.astype(F32)

    own = -joined(face(d_high, 0, 1), face(d_low, 0, 1))
    other = -joined(face(d_high, 1, 1), face(d_low, 1, 1))
    across = joined(last_high[...], last_low[...])
    rows = slot_map(flag, own, other, across, True)
    for s in (0, 1):
        high[s], low[s] = two(rows[s])
        far_high[s], far_low[s] = two(through(high[s], low[s], depth, passes))


def last_base_kernel(flags, line, second_line, high, low, inflow, out):
    flag = flags[0:1, :] > 0.5
    entered = spread(inflow[...])
    out[0] = pick(flag, second_line[...], line[...]) + map_times(high[0], low[0], entered)
    out[1] = pick(flag, line[...], second_line[...]) + map_times(high[1], low[1], entered)


def last_kernel(stride, backward, base, high, low, arrived, out):
    entered = spread(last_arrived(stride, backward, arrived))
    for s in (0, 1):
        out[s] = base[s] + map_times(high[s], low[s], entered)


def digit_of(size, stride):
    return lax.rem(lax.div(lax.axis_index("stream"), stride), size)


def place_of(size, stride, backward):
    digit = digit_of(size, stride)
    return size - 1 - digit if backward else digit


def source_place(size, stride, backward, k):
    digit = digit_of(size, stride)
    m = digit ^ k if size & (size - 1) == 0 else lax.rem(digit - k + size, size)
    return size - 1 - m if backward else m


def store_packed(high, low, m, packed, backward):
    width = packed.shape[0] // 2
    a, b, c, flag = unpack_map(packed[:width], packed[width:])
    for s, row in enumerate(slot_map(flag, a, b, c, backward)):
        high[m, s * width : (s + 1) * width], low[m, s * width : (s + 1) * width] = two(row)


def in_turn(size, place, values, high, low):
    state = values[0]
    below = jnp.zeros_like(state)
    for m in range(1, size):
        below = jnp.where(place == m, state, below)
        if m < size:
            state = values[m] + map_times(high[m], low[m], spread(state))
    return state, below


def fold_kernel(size, stride, backward, first, steps, *refs):
    parts, refs = refs[:size], refs[size:]
    if first:
        total, before, high, low, held = refs
    else:
        high, low, total, before, held = refs
    rows = total.shape[0]
    for k, part in zip(steps, parts):
        m = source_place(size, stride, backward, k)
        held[m] = part[:rows, :]
        if first == "packed":
            store_packed(high, low, m, part[rows:, :], backward)
        elif first:
            for f in (0, 1):
                a, b = two(part[rows * (1 + f) : rows * (2 + f), :])
                high[m, :, f * LANES : (f + 1) * LANES] = a
                low[m, :, f * LANES : (f + 1) * LANES] = b
    place = place_of(size, stride, backward)
    total[...], before[...] = in_turn(size, place, held, high, low)


def unpack_kernel(size, stride, backward, steps, *refs):
    parts, (high, low) = refs[:size], refs[size:]
    for k, part in zip(steps, parts):
        store_packed(high, low, source_place(size, stride, backward, k), part[...], backward)


def total_kernel(size, stride, backward, steps, *refs):
    parts, (high, low, total, held) = refs[:size], refs[size:]
    for k, part in zip(steps, parts):
        held[source_place(size, stride, backward, k)] = part[...]
    below = jnp.concatenate([spread(held[m]) for m in range(size - 1)], axis=0)
    total[...] = held[size - 1] + map_times(high[...], low[...], below)


def before_kernel(size, stride, backward, held, high, low, before):
    place = place_of(size, stride, backward)
    _, before[...] = in_turn(size, place, held, high, low)


def suffix_kernel(size, high, low, out_high, out_low):
    state_high, state_low = high[size - 1], low[size - 1]
    for m in reversed(range(size - 1)):
        lanes = slice(2 * LANES * m, 2 * LANES * (m + 1))
        out_high[:, lanes], out_low[:, lanes] = state_high, state_low
        if m:
            inner = high[m].astype(F32) + low[m].astype(F32)
            state_high, state_low = two(map_times(state_high, state_low, spread(inner)))


def passage_kernel(size, stride, backward, high, low, pass_high, pass_low, whole):
    rows = high.shape[1]
    width = rows // 2
    place = place_of(size, stride, backward)
    row = lax.broadcasted_iota(jnp.int32, (rows, 2 * LANES), 0)
    lane = lax.broadcasted_iota(jnp.int32, (rows, 2 * LANES), 1)
    moved = jnp.where(row < width, row, row - width + LANES)
    state = jnp.where(moved == lane, 1.0, 0.0)
    kept = state
    for m in range(size):
        kept = jnp.where(place == m, state, kept)
        if m < size - 1 or whole is not None:
            if m:
                state = map_times(high[m], low[m], spread(state))
            else:
                state = high[0].astype(F32) + low[0].astype(F32)
    pass_high[...], pass_low[...] = two(kept)
    if whole is not None:
        whole[:rows, :] = state[:, :LANES]
        whole[rows:, :] = state[:, LANES:]


def through(high, low, depth, passes):
    state = None
    for level in range(depth):
        if state is not None:
            high, low = two(state)
        inner = passes[2 * level][...].astype(F32) + passes[2 * level + 1][...].astype(F32)
        state = map_times(high, low, spread(inner))
    return high.astype(F32) + low.astype(F32) if state is None else state


def join_kernel(depth, side_high, side_low, *refs):
    passes, (high, low) = refs[:-2], refs[-2:]
    rows = side_high.shape[0]
    high[:rows], low[:rows] = two(through(side_high[...], side_low[...], depth, passes))
    if depth == 1:
        high[rows:], low[rows:] = passes[0][...], passes[1][...]
    else:
        high[rows:], low[rows:] = two(through(passes[0][...], passes[1][...], depth - 1, passes[2:]))


def base_kernel(depth, *refs):
    befores, refs = refs[:depth], refs[depth:]
    passes, refs = refs[: 2 * depth], refs[2 * depth :]
    side, high, low, base, inflow = refs
    state = befores[depth - 1][...]
    for level in reversed(range(depth - 1)):
        inner = map_times(passes[2 * level][...], passes[2 * level + 1][...], spread(state))
        state = befores[level][...] + inner
    inflow[...] = state
    if base is not None:
        both = map_times(high[...], low[...], spread(state))
        rows = state.shape[0]
        base[0] = side[0] + both[:rows]
        base[1] = side[1] + both[rows:]


def last_arrived(stride, backward, arrived):
    if not stride:
        return jnp.zeros(arrived.shape, F32)
    upper = digit_of(2, stride) == (0 if backward else 1)
    return jnp.where(upper, arrived[...], 0.0)


def enter_kernel(stride, backward, involution, base, before, high, low, arrived,
                 inflow, first, second):
    rows = inflow.shape[0]
    entered = spread(last_arrived(stride, backward, arrived))
    added = map_times(high[...], low[...], entered)
    inflow[...] = before[...] + added[2 * rows :]
    lower_face = base[0] + added[:rows]
    upper_face = base[1] + added[rows : 2 * rows]
    if involution:
        odd = lax.rem(lax.axis_index("span"), 2) == 1
        first[...] = pick(odd, lower_face, upper_face)
        second[...] = pick(odd, upper_face, lower_face)
    else:
        first[...] = upper_face
        second[...] = lower_face


def levels_of(count):
    sizes, left = [], count
    for factor in (4, 2):
        while left % factor == 0:
            sizes.append(factor)
            left //= factor
    factor = 3
    while left > 1:
        while left % factor == 0:
            sizes.insert(0, factor)
            left //= factor
        factor += 2
    strides, stride = [], 1
    for size in sizes:
        strides.append(stride)
        stride *= size
    return list(zip(sizes, strides))


def steps_of(size):
    return (0, 2, 1, 3) if size == 4 else tuple(range(size))


def exchange(block, axis, size, stride, k):
    pairs = []
    for i in range(lax.axis_size(axis)):
        digit = (i // stride) % size
        target = digit ^ k if size & (size - 1) == 0 else (digit + k) % size
        pairs.append((i, i + (target - digit) * stride))
    return lax.ppermute(block, axis, pairs)


def side_exchange(first, second, involution):
    n = lax.axis_size("span")
    if involution:
        pairs = [(j, j ^ 1) for j in range(n)]
        across = [(j, (j + 1) % n if j % 2 else (j - 1) % n) for j in range(n)]
        second = lax.ppermute(second, "span", across)
        first = lax.ppermute(first, "span", pairs)
        return first, second
    return (
        lax.ppermute(first, "span", [(j, (j + 1) % n) for j in range(n)]),
        lax.ppermute(second, "span", [(j, (j - 1) % n) for j in range(n)]),
    )


def local(rhs, inv_blocks, coupling, trace_ops, lift_ops, order, counts, neighbours, face_ids):
    source, inverse_in = rhs[0, 0], inv_blocks[0, 0]
    slots, block, columns = source.shape
    faces, width = trace_ops.shape[:2]
    links = neighbours.shape[-1]
    rows = 2 * width
    if slots != 2 or columns % LANES or 3 * width >= 2 * LANES:
        raise ValueError("unsupported sizes")
    levels = levels_of(lax.axis_size("stream"))
    span = lax.axis_size("span")
    involution = span % 2 == 0 and span > 2

    field, trace = shape(block, columns), shape(rows, columns)
    unit = 2 * block * block * LANES
    hbm = pl.BlockSpec(memory_space=pl.ANY)
    given = (order[0, 0], counts[0], neighbours[0, 0], face_ids[0, 0], source, inverse_in, coupling,
           trace_ops, jnp.swapaxes(lift_ops, 1, 2))
    inputs = tuple(
        x if x.size == 1 else pltpu.with_memory_space_constraint(x, pltpu.HBM) for x in given
    )
    packed, flags = call(
        first_kernel,
        [shape(2 * rows, LANES), shape(8 * -(-(2 + 2 * links) // 8), LANES)],
        inputs,
        20 * unit,
        [
            pltpu.VMEM((2, block, block), BF16),
            pltpu.VMEM((links, block, block), BF16),
            pltpu.VMEM((width, block), BF16),
            pltpu.VMEM((LANES, block), BF16),
            pltpu.VMEM((2, block, columns), F32),
            *(pltpu.SMEM(x.shape, jnp.int32) for x in inputs[:4]),
            pltpu.SemaphoreType.DMA((4,)),
            pltpu.SemaphoreType.DMA((4,)),
            pltpu.SemaphoreType.DMA((links,)),
        ],
        [hbm] * len(inputs),
    )
    table, square = pair(2, block, faces * LANES), pair(2, block, block)
    side_pair, line_pair = pair(2 * rows, 2 * LANES), pair(rows, 4 * LANES)
    store = {}

    def maps():
        held = (inputs[0], *inputs[3:])
        return call(
            maps_kernel,
            [shape(*trace_ops.shape, dtype=BF16), shape(2, block, columns), *table, *square,
             shape(2, rows, columns), *side_pair, shape(rows, LANES), *line_pair,
             *pair(block, LANES)],
            (*held, flags),
            50 * unit,
            [
                pltpu.VMEM((2, block, block), BF16),
                pltpu.VMEM((2, block, columns), F32),
                pltpu.VMEM((faces * LANES, block), BF16),
                pltpu.VMEM((2, links, block, block), BF16),
                *(pltpu.SMEM(x.shape, jnp.int32) for x in held[:2]),
                pltpu.SemaphoreType.DMA((2,)),
                pltpu.SemaphoreType.DMA((3 + faces + 2 * links,)),
            ],
            [hbm] * len(held) + [pl.BlockSpec(memory_space=pltpu.VMEM)],
        )

    def more_maps():
        return call(
            more_maps_kernel,
            [*side_pair, *line_pair],
            (flags, traces, *store["d"], *store["e"], *store["last"]),
            16 * unit,
        )

    def parts_of(block, size, stride, steps):
        return [block] + [exchange(block, "stream", size, stride, k) for k in steps[1:]]

    def passage(key, size, stride):
        backward, level = key
        body = partial(passage_kernel, size, stride, backward)
        if level == len(levels) - 1 or (level == len(levels) - 2 and levels[-1][0] == 2):
            body, outs = partial(lambda f, *refs: f(*refs, None), body), []
        else:
            outs = [shape(2 * rows, LANES)]
        high, low, *whole = call(body, pair(rows, 2 * LANES) + outs, store["maps", key], 2 * unit)
        store["pass", key] = (high, low)
        store["whole", key] = whole

    def carried(total, backward, beside):
        befores, passes, done, stride_of_last = [], [], None, 0
        for level, (size, stride) in enumerate(levels):
            key = (backward, level)
            if level == len(levels) - 1 and size == 2:
                total, stride_of_last = exchange(total, "stream", size, stride, 1), stride
                break
            first = ("maps", key) not in store
            if first:
                first = "whole" if level else "packed"
                if level:
                    total = jnp.concatenate([total, *store["whole", (backward, level - 1)]], axis=0)
            steps = steps_of(size)
            parts = parts_of(total, size, stride, steps)
            if level == 0:
                parts, done = lax.optimization_barrier((parts, beside()))
            held = shape(size, rows, columns)
            scratch = [pltpu.VMEM(held.shape, F32)]
            body = partial(fold_kernel, size, stride, backward, first, steps)
            if first:
                outs = [trace, trace, *pair(size, rows, 2 * LANES)]
                total, before, *kept = call(body, outs, parts, unit, scratch)
                store["maps", key] = tuple(kept)
                passage(key, size, stride)
            elif ("suffix", key) in store:
                body = partial(total_kernel, size, stride, backward, steps)
                total, held = call(body, [trace, held], (*parts, *store["suffix", key]), unit)
                body = partial(before_kernel, size, stride, backward)
                (before,) = call(body, [trace], (held, *store["maps", key]), unit)
            else:
                ins = (*parts, *store["maps", key])
                total, before = call(body, [trace, trace], ins, unit, scratch)
            befores.append(before)
            passes += store["pass", key]
        if not befores:
            befores = [jnp.zeros_like(total)]
            passes = [jnp.zeros((rows, 2 * LANES), BF16)] * 2
        return befores, passes, total, stride_of_last, done or beside()

    def suffixes(backward):
        out = {}
        for level, (size, _) in enumerate(levels):
            key = (backward, level)
            if ("maps", key) in store:
                outs = pair(rows, 2 * LANES * (size - 1))
                out["suffix", key] = call(
                    partial(suffix_kernel, size), outs, store["maps", key], unit
                )
        return out

    def send_maps(block):
        size, stride = levels[0]
        after = store["pass", (False, 0)]
        block, store["pass", (False, 0)] = lax.optimization_barrier((block, after))
        return parts_of(block, size, stride, steps_of(size))

    def take_maps(parts):
        size, stride = levels[0]
        body = partial(unpack_kernel, size, stride, True, steps_of(size))
        store["maps", (True, 0)] = tuple(call(body, pair(size, rows, 2 * LANES), parts, unit))
        passage((True, 0), size, stride)

    grouped = levels and not (len(levels) == 1 and levels[0][0] == 2)
    halves = [backward for _ in range(SWEEPS) for backward in (False, True)]
    for number, backward in enumerate(halves):
        final = number == len(halves) - 1
        if number == 0:
            befores, passes, arrived, stride, done = carried(packed, backward, maps)
            traces, *done = done
            store["z"], store["d"], store["e"], side = done[0], done[1:3], done[3:5], done[5]
            store["side", False], store["line", True] = done[6:8], done[9:11]
            store["last"] = done[11:13]
            line = store["z"][0]
            if grouped:
                sent = send_maps(done[8])
        else:
            (outflow,) = call(
                partial(outflow_kernel, involution),
                [trace],
                (base, *store["line", backward], first, second),
                unit,
            )
            body = partial(field_kernel, backward, involution)
            outs = [field, field] if final else [field, shape(2, rows, columns)]
            ins = (flags, first, second, start, left, *store["d"], *store["e"], traces)
            cut = len(ins) + (2 if final else 1)
            body = partial(lambda f, n, *refs: f(*refs[:n], None, *refs[n:]), body, cut)

            def beside():
                more = {}
                if number == 1:
                    out = more_maps()
                    more = {("side", True): out[:2], ("line", False): out[2:]}
                return call(body, outs, ins, 14 * unit), more

            if number == 1 and grouped:
                take_maps(sent)
                store.update(suffixes(True))
            befores, passes, arrived, stride, done = carried(outflow, backward, beside)
            line, side = done[0]
            store.update(done[1])
        depth = len(befores)
        if final:
            wide = pair(2, block, 2 * LANES)
            body = partial(last_response_kernel, depth)
            out = call(body, wide + wide, (flags, *store["d"], *store["last"], *passes), 4 * unit)
            near, far = out[:2], out[2:]
            body = partial(base_kernel, depth)
            body = partial(lambda f, *refs: f(*refs[:-1], None, None, None, None, refs[-1]), body)
            (before,) = call(body, [trace], (*befores, *passes), unit)
            ins = (flags, line, side, *near, before)
            (base,) = call(last_base_kernel, [shape(2, block, columns)], ins, 2 * unit)
            body = partial(last_kernel, stride, backward)
            (x,) = call(body, [shape(2, block, columns)], (base, *far, arrived), 2 * unit)
            break
        if number == 0:
            store.update(suffixes(False))
        if ("join", backward) not in store:
            ins = (*store["side", backward], *passes)
            body = partial(join_kernel, depth)
            store["join", backward] = call(body, pair(3 * rows, 2 * LANES), ins, unit)
        base, before = call(
            partial(base_kernel, depth),
            [shape(2, rows, columns), trace],
            (*befores, *passes, side, *store["side", backward]),
            unit,
        )
        inflow, first, second = call(
            partial(enter_kernel, stride, backward, involution),
            [trace] * 3,
            (base, before, *store["join", backward], arrived),
            unit,
        )
        first, second = side_exchange(first, second, involution)
        base, start, left = call(
            partial(prepare_kernel, backward),
            [trace, field, field],
            (flags, inflow, line, store["z"], *store["d"], *store["e"], traces),
            14 * unit,
        )
    return x[None, None]


def solution(mesh):
    placed = (
        P("stream", "span", None, None, None),
        P("stream", "span", None, None, None),
        P(),
        P(),
        P(),
        P("stream", "span", None),
        P("stream", "span"),
        P("stream", "span", None, None),
        P("stream", "span", None, None),
    )
    return jax.shard_map(
        local,
        mesh=mesh,
        in_specs=placed,
        out_specs=P("stream", "span", None, None, None),
        check_vma=False,
    )
```

```python
from functools import partial

import jax
import jax.numpy as jnp
from jax import lax
from jax.experimental import pallas as pl
from jax.experimental.pallas import tpu as pltpu
from jax.sharding import PartitionSpec as P

SWEEPS = 2
LANES = 128
F32 = jnp.float32
BF16 = jnp.bfloat16


def mm(a, b):
    return jnp.dot(a, b, preferred_element_type=F32)


def mm_t(a, b):
    return lax.dot_general(a, b, (((1,), (1,)), ((), ())), preferred_element_type=F32)


def two(x):
    high = x.astype(BF16)
    low = (x - high.astype(F32)).astype(BF16)
    return high, low


def exact_times(operator, x):
    n = x.shape[1]
    both = mm(operator, jnp.concatenate(two(x), axis=1))
    return both[:, :n] + both[:, n:]


def map_times(high, low, x):
    n = x.shape[1]
    x_high, x_low = two(x)
    both = mm(high, jnp.concatenate([x_high, x_low], axis=1))
    return both[:, :n] + both[:, n:] + mm(low, x_high)


def pad_rows(x):
    gap = jnp.zeros((LANES - x.shape[0], x.shape[1]), x.dtype)
    return jnp.concatenate([x, gap], axis=0)


def spread(x):
    width = x.shape[0] // 2
    return jnp.concatenate([pad_rows(x[:width]), pad_rows(x[width:])], axis=0)


def pick(flag, yes, no):
    return jnp.where(flag, yes, no)


def by_position(flag, x):
    width = x.shape[0] // 2
    return (
        pad_rows(pick(flag, x[:width], x[width:])),
        pad_rows(pick(flag, x[width:], x[:width])),
    )


def slot_map(flag, first, second, across, backward):
    none = jnp.zeros_like(across)
    if backward:
        lower, upper = pick(flag, none, across), pick(flag, across, none)
    else:
        lower, upper = pick(flag, across, none), pick(flag, none, across)
    return (
        jnp.concatenate([pick(flag, first, second), upper], axis=1),
        jnp.concatenate([lower, pick(flag, second, first)], axis=1),
    )


def pack_map(first, second, across, flag_value):
    width = first.shape[0]
    spare = LANES - width
    lane = lax.broadcasted_iota(jnp.int32, first.shape, 1)
    one = jnp.where(lane >= width, pltpu.roll(across, width, 1), first)
    rest = jnp.where(lane >= width, pltpu.roll(across, width - spare, 1), second)
    return one, jnp.where(lane >= 2 * width - spare, flag_value, rest)


def unpack_map(one, two_):
    width = one.shape[0]
    spare = LANES - width
    lane = lax.broadcasted_iota(jnp.int32, one.shape, 1)
    none = jnp.zeros_like(one)
    first = jnp.where(lane < width, one, none)
    second = jnp.where(lane < width, two_, none)
    across = jnp.where(lane < spare, pltpu.roll(one, LANES - width, 1), none)
    rest = pltpu.roll(two_, LANES - (width - spare), 1)
    across = jnp.where((lane >= spare) & (lane < width), rest, across)
    flag = jnp.broadcast_to(two_[0:1, LANES - 1 : LANES], (1, LANES)) > 0.5
    return first, second, across, flag


def call(body, outs, ins, flops=0, scratch=(), spaces=None):
    vmem = pl.BlockSpec(memory_space=pltpu.VMEM)
    moved = sum(x.size * x.dtype.itemsize for x in ins)
    moved += sum(o.size * o.dtype.itemsize for o in outs)
    return pl.pallas_call(
        body,
        out_shape=list(outs),
        in_specs=spaces or [vmem] * len(ins),
        out_specs=[vmem] * len(outs),
        scratch_shapes=list(scratch),
        compiler_params=pltpu.CompilerParams(vmem_limit_bytes=24 * 2**20),
        cost_estimate=pl.CostEstimate(flops=flops, bytes_accessed=moved, transcendentals=0),
    )(*ins)


def shape(*dims, dtype=F32):
    return jax.ShapeDtypeStruct(dims, dtype)


def pair(*dims):
    return [shape(*dims, dtype=BF16)] * 2


def face(ref, q, f, count=1):
    return ref[q, :, f * LANES : (f + count) * LANES]


def lift_times(high, low, q, f, x, count=1):
    return map_times(face(high, q, f, count), face(low, q, f, count), x)


def times_exact(x, operator):
    n = x.shape[0]
    both = mm(jnp.concatenate(two(x), axis=0), operator)
    return both[:n] + both[n:]


def first_kernel(order_in, count_in, links_in, types_in, rhs_in, inverse_in, table_in, traces_in,
                 lifts_in, packed, flags, inverse, blocks, trace, head, rhs, order, count, links,
                 types, small, large, own):
    faces = blocks.shape[0]
    width = trace.shape[0]
    columns = rhs.shape[2]
    scalars = [
        pltpu.make_async_copy(a, b, small.at[i])
        for i, (a, b) in enumerate(
            ((order_in, order), (types_in, types), (links_in, links), (count_in, count))
        )
    ]
    pairs = [
        (traces_in.at[1], trace),
        (inverse_in, inverse),
        (lifts_in.at[0], head.at[pl.ds(0, width), :]),
        (rhs_in, rhs),
    ]
    copies = [pltpu.make_async_copy(a, b, large.at[i]) for i, (a, b) in enumerate(pairs)]
    for c in scalars + copies:
        c.start()
    gap = head.at[pl.ds(width, LANES - width), :]
    gap[...] = jnp.zeros(gap.shape, BF16)
    flags[...] = jnp.zeros_like(flags)
    for c in scalars:
        c.wait()
    a, b = order[0], order[1]
    fetched = [
        pltpu.make_async_copy(table_in.at[types[b, m]], blocks.at[m], own.at[m])
        for m in range(faces)
    ]
    for c in fetched:
        c.start()
    alive = (count[0] > 1).astype(F32)
    flags[0:1, :] = jnp.full((1, LANES), (a == 0).astype(F32))
    flags[1:2, :] = jnp.full((1, LANES), alive)
    for q, s in enumerate((a, b)):
        for m in range(faces):
            row = 2 + q * faces + m
            flags[row : row + 1, :] = jnp.full((1, LANES), (links[s, m] < 2).astype(F32))
    copies[0].wait()
    copies[1].wait()
    far = mm(trace[...], inverse[b]) * alive
    far_high, far_low = two(far)
    copies[2].wait()
    lifted = mm_t(far_high, head[...]) + mm_t(far_low, head[...])
    answer = mm_t(inverse[a], head[...])
    copies[3].wait()
    start = jnp.concatenate([exact_times(inverse[a], rhs[a]), answer], axis=1)
    near = exact_times(trace[...], start)
    packed[pl.ds(pl.multiple_of(a * width, 8), width), :] = near[:, :columns]
    shown = map_times(far_high, far_low, rhs[b])
    met = None
    for m in range(faces):
        fetched[m].wait()
        product = times_exact(far, blocks[m]) * (links[b, m] < 2).astype(F32)
        met = product if met is None else met + product
    met_high, met_low = two(met)
    met = map_times(met_high, met_low, start)
    packed[pl.ds(pl.multiple_of(b * width, 8), width), :] = shown - met[:, :columns]
    one, rest = pack_map(-near[:, columns:], -lifted, met[:, columns:], flags[0:1, :])
    packed[2 * width : 3 * width, :] = one
    packed[3 * width : 4 * width, :] = rest


def side_traces(out, traces, flag, first, second):
    width = traces.shape[1]
    n = first.shape[1]
    for f in (2, 3):
        shown = exact_times(traces[f], jnp.concatenate([first, second], axis=1))
        out[f - 2, :width, :] = pick(flag, shown[:, :n], shown[:, n:])
        out[f - 2, width:, :] = pick(flag, shown[:, n:], shown[:, :n])


def store_side_map(high, low, traces, flag, first, second, across, backward):
    width = traces.shape[1]
    for f in (2, 3):
        shown = exact_times(traces[f], jnp.concatenate([first, second, across], axis=1))
        rows = slot_map(
            flag, -shown[:, :LANES], -shown[:, LANES : 2 * LANES], shown[:, 2 * LANES :], backward
        )
        for s in (0, 1):
            place = ((f - 2) * 2 + s) * width
            high[place : place + width, :], low[place : place + width, :] = two(rows[s])


def store_line_map(high, low, flag, first, second, across, backward):
    width = first.shape[0]
    for f in (0, 1):
        lanes = slice(f * LANES, (f + 1) * LANES)
        rows = slot_map(flag, -first[:, lanes], -second[:, lanes], across[:, lanes], backward)
        for s in (0, 1):
            place, held = slice(s * width, (s + 1) * width), slice(2 * f * LANES, 2 * (f + 1) * LANES)
            high[place, held], low[place, held] = two(rows[s])


def maps_kernel(order_in, types_in, rhs_in, inverse_in, table_in, traces_in, lifts_in, flags,
                traces, z, d_high, d_low, e_high, e_low, side, side_high, side_low, back_map,
                q_high, q_low, last_high, last_low,
                inverse, rhs, lifts, blocks, order, types, small, large):
    width = traces.shape[1]
    links = blocks.shape[1]
    pairs = [(inverse_in, inverse), (rhs_in, rhs), (traces_in, traces)]
    for f in range(lifts_in.shape[0]):
        pairs.append((lifts_in.at[f], lifts.at[pl.ds(f * LANES, width), :]))
    scalars = [
        pltpu.make_async_copy(order_in, order, small.at[0]),
        pltpu.make_async_copy(types_in, types, small.at[1]),
    ]
    copies = [pltpu.make_async_copy(a, b, large.at[i]) for i, (a, b) in enumerate(pairs)]
    for c in scalars + copies:
        c.start()
    for f in range(lifts_in.shape[0]):
        gap = lifts.at[pl.ds(f * LANES + width, LANES - width), :]
        gap[...] = jnp.zeros(gap.shape, BF16)
    for c in scalars:
        c.wait()
    own = [
        pltpu.make_async_copy(
            table_in.at[types[order[q], m]], blocks.at[q, m], large.at[len(pairs) + q * links + m]
        )
        for q in (0, 1)
        for m in range(links)
    ]
    for c in own:
        c.start()
    for c in copies + own:
        c.wait()
    flag = flags[0:1, :] > 0.5
    for q in (0, 1):
        s = order[q]
        scale = flags[1:2, 0:1] if q else 1.0
        z[q] = exact_times(inverse[s], rhs[s]) * scale
        d_high[q], d_low[q] = two(mm_t(inverse[s], lifts[...]) * scale)
        total = None
        for m in range(links):
            row = 2 + q * links + m
            block = blocks[q, m].astype(F32) * flags[row : row + 1, 0:1]
            total = block if total is None else total + block
        high, low = two(total)
        e_high[q], e_low[q] = two((mm(inverse[s], high) + mm(inverse[s], low)) * scale)

    def lift_of(q):
        return face(d_high, q, 0).astype(F32) + face(d_low, q, 0).astype(F32)

    n = z.shape[2]
    met = jnp.concatenate([z[0], lift_of(0)], axis=1)
    met = map_times(e_high[1], e_low[1], met)
    side_traces(side, traces, flag, z[0], z[1] - met[:, :n])
    store_side_map(
        side_high, side_low, traces, flag, lift_of(0), lift_of(1), met[:, n:], False
    )
    faces = lifts.shape[0] // LANES - 1
    high, low = face(d_high, 1, 1, faces), face(d_low, 1, 1, faces)
    both = mm(e_high[0], jnp.concatenate([high, low], axis=1))
    n = faces * LANES
    across = both[:, :n] + both[:, n:] + mm(e_low[0], high)
    last_high[...], last_low[...] = two(across[:, :LANES])
    shown = []
    for q in (0, 1):
        shown.append(
            mm(traces[0], face(d_high, q, 1, faces)) + mm(traces[0], face(d_low, q, 1, faces))
        )
    shown.append(exact_times(traces[0], across))
    one, rest = pack_map(
        -shown[0][:, :LANES], -shown[1][:, :LANES], shown[2][:, :LANES], flags[0:1, :]
    )
    back_map[:width, :] = one
    back_map[width:, :] = rest
    store_line_map(q_high, q_low, flag, *(s[:, LANES:] for s in shown), True)


def more_maps_kernel(flags, traces, d_high, d_low, e_high, e_low, last_high, last_low,
                     side_high, side_low, q_high, q_low):
    flag = flags[0:1, :] > 0.5

    def joined(q, f, count):
        return face(d_high, q, f, count).astype(F32) + face(d_low, q, f, count).astype(F32)

    across = last_high[...].astype(F32) + last_low[...].astype(F32)
    store_side_map(
        side_high, side_low, traces, flag, joined(0, 1, 1), joined(1, 1, 1), across, True
    )
    high, low = face(d_high, 0, 2, 2), face(d_low, 0, 2, 2)
    both = mm(e_high[1], jnp.concatenate([high, low], axis=1))
    n = 2 * LANES
    across = both[:, :n] + both[:, n:] + mm(e_low[1], high)
    shown = exact_times(
        traces[1], jnp.concatenate([joined(0, 2, 2), joined(1, 2, 2), across], axis=1)
    )
    store_line_map(
        q_high, q_low, flag, shown[:, :n], shown[:, n : 2 * n], shown[:, 2 * n :], False
    )


def prepare_kernel(backward, flags, inflow, line, z, d_high, d_low, e_high, e_low, traces,
                   outflow, field, other):
    p0, p1 = (1, 0) if backward else (0, 1)
    f = 1 if backward else 0
    flag = flags[0:1, :] > 0.5
    entered = by_position(flag, inflow[...])
    width = traces.shape[1]
    lifted = lift_times(d_high, d_low, p0, f, entered[p0])
    y = line[...] - lifted
    start = z[p1] - lift_times(d_high, d_low, p1, f, entered[p1])
    start = start - map_times(e_high[p1], e_low[p1], y)
    field[...] = start
    left = z[p0] - lifted
    other[...] = left
    end = left - map_times(e_high[p0], e_low[p0], start)
    fields = (start, end) if p1 == 0 else (end, start)
    n = start.shape[1]
    shown = exact_times(traces[1 if backward else 0], jnp.concatenate(fields, axis=1))
    outflow[:width, :] = pick(flag, shown[:, :n], shown[:, n:])
    outflow[width:, :] = pick(flag, shown[:, n:], shown[:, :n])


def sides(involution, first, second):
    if not involution:
        return first[...], second[...]
    odd = lax.rem(lax.axis_index("span"), 2) == 1
    return pick(odd, first[...], second[...]), pick(odd, second[...], first[...])


def outflow_kernel(involution, base, q_high, q_low, first, second, outflow):
    arrived = jnp.concatenate([spread(v) for v in sides(involution, first, second)], axis=0)
    outflow[...] = base[...] + map_times(q_high[...], q_low[...], arrived)


def field_kernel(backward, involution, flags, first, second, start, left, d_high, d_low, e_high,
                 e_low, traces, line, second_line, side):
    p0, p1 = (1, 0) if backward else (0, 1)
    flag = flags[0:1, :] > 0.5
    arrived = [by_position(flag, v) for v in sides(involution, first, second)]

    def lifted(q):
        both = jnp.concatenate([v[q] for v in arrived], axis=0)
        return lift_times(d_high, d_low, q, 2, both, 2)

    y0 = start[...] - lifted(p0)
    line[...] = y0
    y1 = left[...] - lifted(p1) - map_times(e_high[p1], e_low[p1], y0)
    if second_line is not None:
        second_line[...] = y1
    if side is not None:
        fields = (y1, y0) if backward else (y0, y1)
        side_traces(side, traces, flag, *fields)


def last_response_kernel(depth, flags, d_high, d_low, last_high, last_low, *refs):
    passes, (high, low, far_high, far_low) = refs[:-4], refs[-4:]
    flag = flags[0:1, :] > 0.5
    none = jnp.zeros((d_high.shape[1], LANES), F32)

    def joined(h, l):
        return h.astype(F32) + l.astype(F32)

    own = -joined(face(d_high, 0, 1), face(d_low, 0, 1))
    other = -joined(face(d_high, 1, 1), face(d_low, 1, 1))
    across = joined(last_high[...], last_low[...])
    rows = slot_map(flag, own, other, across, True)
    for s in (0, 1):
        high[s], low[s] = two(rows[s])
        far_high[s], far_low[s] = two(through(high[s], low[s], depth, passes))


def last_base_kernel(flags, line, second_line, high, low, inflow, out):
    flag = flags[0:1, :] > 0.5
    entered = spread(inflow[...])
    out[0] = pick(flag, second_line[...], line[...]) + map_times(high[0], low[0], entered)
    out[1] = pick(flag, line[...], second_line[...]) + map_times(high[1], low[1], entered)


def last_kernel(stride, backward, base, high, low, arrived, out):
    entered = spread(last_arrived(stride, backward, arrived))
    for s in (0, 1):
        out[s] = base[s] + map_times(high[s], low[s], entered)


def digit_of(size, stride):
    return lax.rem(lax.div(lax.axis_index("stream"), stride), size)


def place_of(size, stride, backward):
    digit = digit_of(size, stride)
    return size - 1 - digit if backward else digit


def source_place(size, stride, backward, k):
    digit = digit_of(size, stride)
    m = digit ^ k if size & (size - 1) == 0 else lax.rem(digit - k + size, size)
    return size - 1 - m if backward else m


def store_packed(high, low, m, packed, backward):
    width = packed.shape[0] // 2
    a, b, c, flag = unpack_map(packed[:width], packed[width:])
    for s, row in enumerate(slot_map(flag, a, b, c, backward)):
        high[m, s * width : (s + 1) * width], low[m, s * width : (s + 1) * width] = two(row)


def in_turn(size, place, values, high, low):
    state = values[0]
    below = jnp.zeros_like(state)
    for m in range(1, size):
        below = jnp.where(place == m, state, below)
        if m < size:
            state = values[m] + map_times(high[m], low[m], spread(state))
    return state, below


def fold_kernel(size, stride, backward, first, steps, *refs):
    parts, refs = refs[:size], refs[size:]
    if first:
        total, before, high, low, held = refs
    else:
        high, low, total, before, held = refs
    rows = total.shape[0]
    for k, part in zip(steps, parts):
        m = source_place(size, stride, backward, k)
        held[m] = part[:rows, :]
        if first == "packed":
            store_packed(high, low, m, part[rows:, :], backward)
        elif first:
            for f in (0, 1):
                a, b = two(part[rows * (1 + f) : rows * (2 + f), :])
                high[m, :, f * LANES : (f + 1) * LANES] = a
                low[m, :, f * LANES : (f + 1) * LANES] = b
    place = place_of(size, stride, backward)
    total[...], before[...] = in_turn(size, place, held, high, low)


def unpack_kernel(size, stride, backward, steps, *refs):
    parts, (high, low) = refs[:size], refs[size:]
    for k, part in zip(steps, parts):
        store_packed(high, low, source_place(size, stride, backward, k), part[...], backward)


def total_kernel(size, stride, backward, steps, *refs):
    parts, (high, low, total, held) = refs[:size], refs[size:]
    for k, part in zip(steps, parts):
        held[source_place(size, stride, backward, k)] = part[...]
    below = jnp.concatenate([spread(held[m]) for m in range(size - 1)], axis=0)
    total[...] = held[size - 1] + map_times(high[...], low[...], below)


def before_kernel(size, stride, backward, held, high, low, before):
    place = place_of(size, stride, backward)
    _, before[...] = in_turn(size, place, held, high, low)


def suffix_kernel(size, high, low, out_high, out_low):
    state_high, state_low = high[size - 1], low[size - 1]
    for m in reversed(range(size - 1)):
        lanes = slice(2 * LANES * m, 2 * LANES * (m + 1))
        out_high[:, lanes], out_low[:, lanes] = state_high, state_low
        if m:
            inner = high[m].astype(F32) + low[m].astype(F32)
            state_high, state_low = two(map_times(state_high, state_low, spread(inner)))


def passage_kernel(size, stride, backward, high, low, pass_high, pass_low, whole):
    rows = high.shape[1]
    width = rows // 2
    place = place_of(size, stride, backward)
    row = lax.broadcasted_iota(jnp.int32, (rows, 2 * LANES), 0)
    lane = lax.broadcasted_iota(jnp.int32, (rows, 2 * LANES), 1)
    moved = jnp.where(row < width, row, row - width + LANES)
    state = jnp.where(moved == lane, 1.0, 0.0)
    kept = state
    for m in range(size):
        kept = jnp.where(place == m, state, kept)
        if m < size - 1 or whole is not None:
            if m:
                state = map_times(high[m], low[m], spread(state))
            else:
                state = high[0].astype(F32) + low[0].astype(F32)
    pass_high[...], pass_low[...] = two(kept)
    if whole is not None:
        whole[:rows, :] = state[:, :LANES]
        whole[rows:, :] = state[:, LANES:]


def through(high, low, depth, passes):
    state = None
    for level in range(depth):
        if state is not None:
            high, low = two(state)
        inner = passes[2 * level][...].astype(F32) + passes[2 * level + 1][...].astype(F32)
        state = map_times(high, low, spread(inner))
    return high.astype(F32) + low.astype(F32) if state is None else state


def join_kernel(depth, side_high, side_low, *refs):
    passes, (high, low) = refs[:-2], refs[-2:]
    rows = side_high.shape[0]
    high[:rows], low[:rows] = two(through(side_high[...], side_low[...], depth, passes))
    if depth == 1:
        high[rows:], low[rows:] = passes[0][...], passes[1][...]
    else:
        high[rows:], low[rows:] = two(through(passes[0][...], passes[1][...], depth - 1, passes[2:]))


def base_kernel(depth, *refs):
    befores, refs = refs[:depth], refs[depth:]
    passes, refs = refs[: 2 * depth], refs[2 * depth :]
    side, high, low, base, inflow = refs
    state = befores[depth - 1][...]
    for level in reversed(range(depth - 1)):
        inner = map_times(passes[2 * level][...], passes[2 * level + 1][...], spread(state))
        state = befores[level][...] + inner
    inflow[...] = state
    if base is not None:
        both = map_times(high[...], low[...], spread(state))
        rows = state.shape[0]
        base[0] = side[0] + both[:rows]
        base[1] = side[1] + both[rows:]


def last_arrived(stride, backward, arrived):
    if not stride:
        return jnp.zeros(arrived.shape, F32)
    upper = digit_of(2, stride) == (0 if backward else 1)
    return jnp.where(upper, arrived[...], 0.0)


def enter_kernel(stride, backward, involution, base, before, high, low, arrived,
                 inflow, first, second):
    rows = inflow.shape[0]
    entered = spread(last_arrived(stride, backward, arrived))
    added = map_times(high[...], low[...], entered)
    inflow[...] = before[...] + added[2 * rows :]
    lower_face = base[0] + added[:rows]
    upper_face = base[1] + added[rows : 2 * rows]
    if involution:
        odd = lax.rem(lax.axis_index("span"), 2) == 1
        first[...] = pick(odd, lower_face, upper_face)
        second[...] = pick(odd, upper_face, lower_face)
    else:
        first[...] = upper_face
        second[...] = lower_face


def levels_of(count):
    sizes, left = [], count
    for factor in (4, 2):
        while left % factor == 0:
            sizes.append(factor)
            left //= factor
    factor = 3
    while left > 1:
        while left % factor == 0:
            sizes.insert(0, factor)
            left //= factor
        factor += 2
    strides, stride = [], 1
    for size in sizes:
        strides.append(stride)
        stride *= size
    return list(zip(sizes, strides))


def steps_of(size):
    return (0, 2, 1, 3) if size == 4 else tuple(range(size))


def exchange(block, axis, size, stride, k):
    pairs = []
    for i in range(lax.axis_size(axis)):
        digit = (i // stride) % size
        target = digit ^ k if size & (size - 1) == 0 else (digit + k) % size
        pairs.append((i, i + (target - digit) * stride))
    return lax.ppermute(block, axis, pairs)


def side_exchange(first, second, involution):
    n = lax.axis_size("span")
    if involution:
        pairs = [(j, j ^ 1) for j in range(n)]
        across = [(j, (j + 1) % n if j % 2 else (j - 1) % n) for j in range(n)]
        second = lax.ppermute(second, "span", across)
        first = lax.ppermute(first, "span", pairs)
        return first, second
    return (
        lax.ppermute(first, "span", [(j, (j + 1) % n) for j in range(n)]),
        lax.ppermute(second, "span", [(j, (j - 1) % n) for j in range(n)]),
    )


def local(rhs, inv_blocks, coupling, trace_ops, lift_ops, order, counts, neighbours, face_ids):
    source, inverse_in = rhs[0, 0], inv_blocks[0, 0]
    slots, block, columns = source.shape
    faces, width = trace_ops.shape[:2]
    links = neighbours.shape[-1]
    rows = 2 * width
    if slots != 2 or columns % LANES or 3 * width >= 2 * LANES:
        raise ValueError("unsupported sizes")
    levels = levels_of(lax.axis_size("stream"))
    span = lax.axis_size("span")
    involution = span % 2 == 0 and span > 2

    field, trace = shape(block, columns), shape(rows, columns)
    unit = 2 * block * block * LANES
    hbm = pl.BlockSpec(memory_space=pl.ANY)
    given = (order[0, 0], counts[0], neighbours[0, 0], face_ids[0, 0], source, inverse_in, coupling,
           trace_ops, jnp.swapaxes(lift_ops, 1, 2))
    inputs = tuple(
        x if x.size == 1 else pltpu.with_memory_space_constraint(x, pltpu.HBM) for x in given
    )
    packed, flags = call(
        first_kernel,
        [shape(2 * rows, LANES), shape(8 * -(-(2 + 2 * links) // 8), LANES)],
        inputs,
        20 * unit,
        [
            pltpu.VMEM((2, block, block), BF16),
            pltpu.VMEM((links, block, block), BF16),
            pltpu.VMEM((width, block), BF16),
            pltpu.VMEM((LANES, block), BF16),
            pltpu.VMEM((2, block, columns), F32),
            *(pltpu.SMEM(x.shape, jnp.int32) for x in inputs[:4]),
            pltpu.SemaphoreType.DMA((4,)),
            pltpu.SemaphoreType.DMA((4,)),
            pltpu.SemaphoreType.DMA((links,)),
        ],
        [hbm] * len(inputs),
    )
    table, square = pair(2, block, faces * LANES), pair(2, block, block)
    side_pair, line_pair = pair(2 * rows, 2 * LANES), pair(rows, 4 * LANES)
    store = {}

    def maps():
        held = (inputs[0], *inputs[3:])
        return call(
            maps_kernel,
            [shape(*trace_ops.shape, dtype=BF16), shape(2, block, columns), *table, *square,
             shape(2, rows, columns), *side_pair, shape(rows, LANES), *line_pair,
             *pair(block, LANES)],
            (*held, flags),
            50 * unit,
            [
                pltpu.VMEM((2, block, block), BF16),
                pltpu.VMEM((2, block, columns), F32),
                pltpu.VMEM((faces * LANES, block), BF16),
                pltpu.VMEM((2, links, block, block), BF16),
                *(pltpu.SMEM(x.shape, jnp.int32) for x in held[:2]),
                pltpu.SemaphoreType.DMA((2,)),
                pltpu.SemaphoreType.DMA((3 + faces + 2 * links,)),
            ],
            [hbm] * len(held) + [pl.BlockSpec(memory_space=pltpu.VMEM)],
        )

    def more_maps():
        return call(
            more_maps_kernel,
            [*side_pair, *line_pair],
            (flags, traces, *store["d"], *store["e"], *store["last"]),
            16 * unit,
        )

    def parts_of(block, size, stride, steps):
        return [block] + [exchange(block, "stream", size, stride, k) for k in steps[1:]]

    def passage(key, size, stride):
        backward, level = key
        body = partial(passage_kernel, size, stride, backward)
        if level == len(levels) - 1 or (level == len(levels) - 2 and levels[-1][0] == 2):
            body, outs = partial(lambda f, *refs: f(*refs, None), body), []
        else:
            outs = [shape(2 * rows, LANES)]
        high, low, *whole = call(body, pair(rows, 2 * LANES) + outs, store["maps", key], 2 * unit)
        store["pass", key] = (high, low)
        store["whole", key] = whole

    def carried(total, backward, beside):
        befores, passes, done, stride_of_last = [], [], None, 0
        for level, (size, stride) in enumerate(levels):
            key = (backward, level)
            if level == len(levels) - 1 and size == 2:
                total, stride_of_last = exchange(total, "stream", size, stride, 1), stride
                break
            first = ("maps", key) not in store
            if first:
                first = "whole" if level else "packed"
                if level:
                    total = jnp.concatenate([total, *store["whole", (backward, level - 1)]], axis=0)
            steps = steps_of(size)
            parts = parts_of(total, size, stride, steps)
            if level == 0:
                parts, done = lax.optimization_barrier((parts, beside()))
            held = shape(size, rows, columns)
            scratch = [pltpu.VMEM(held.shape, F32)]
            body = partial(fold_kernel, size, stride, backward, first, steps)
            if first:
                outs = [trace, trace, *pair(size, rows, 2 * LANES)]
                total, before, *kept = call(body, outs, parts, unit, scratch)
                store["maps", key] = tuple(kept)
                passage(key, size, stride)
            elif ("suffix", key) in store:
                body = partial(total_kernel, size, stride, backward, steps)
                total, held = call(body, [trace, held], (*parts, *store["suffix", key]), unit)
                body = partial(before_kernel, size, stride, backward)
                (before,) = call(body, [trace], (held, *store["maps", key]), unit)
            else:
                ins = (*parts, *store["maps", key])
                total, before = call(body, [trace, trace], ins, unit, scratch)
            befores.append(before)
            passes += store["pass", key]
        if not befores:
            befores = [jnp.zeros_like(total)]
            passes = [jnp.zeros((rows, 2 * LANES), BF16)] * 2
        return befores, passes, total, stride_of_last, done or beside()

    def suffixes(backward):
        out = {}
        for level, (size, _) in enumerate(levels):
            key = (backward, level)
            if ("maps", key) in store:
                outs = pair(rows, 2 * LANES * (size - 1))
                out["suffix", key] = call(
                    partial(suffix_kernel, size), outs, store["maps", key], unit
                )
        return out

    def send_maps(block):
        size, stride = levels[0]
        after = store["pass", (False, 0)]
        block, store["pass", (False, 0)] = lax.optimization_barrier((block, after))
        return parts_of(block, size, stride, steps_of(size))

    def take_maps(parts):
        size, stride = levels[0]
        body = partial(unpack_kernel, size, stride, True, steps_of(size))
        store["maps", (True, 0)] = tuple(call(body, pair(size, rows, 2 * LANES), parts, unit))
        passage((True, 0), size, stride)

    grouped = levels and not (len(levels) == 1 and levels[0][0] == 2)
    halves = [backward for _ in range(SWEEPS) for backward in (False, True)]
    for number, backward in enumerate(halves):
        final = number == len(halves) - 1
        if number == 0:
            befores, passes, arrived, stride, done = carried(packed, backward, maps)
            traces, *done = done
            store["z"], store["d"], store["e"], side = done[0], done[1:3], done[3:5], done[5]
            store["side", False], store["line", True] = done[6:8], done[9:11]
            store["last"] = done[11:13]
            line = store["z"][0]
            if grouped:
                sent = send_maps(done[8])
        else:
            (outflow,) = call(
                partial(outflow_kernel, involution),
                [trace],
                (base, *store["line", backward], first, second),
                unit,
            )
            body = partial(field_kernel, backward, involution)
            outs = [field, field] if final else [field, shape(2, rows, columns)]
            ins = (flags, first, second, start, left, *store["d"], *store["e"], traces)
            cut = len(ins) + (2 if final else 1)
            body = partial(lambda f, n, *refs: f(*refs[:n], None, *refs[n:]), body, cut)

            def beside():
                more = {}
                if number == 1:
                    out = more_maps()
                    more = {("side", True): out[:2], ("line", False): out[2:]}
                return call(body, outs, ins, 14 * unit), more

            if number == 1 and grouped:
                take_maps(sent)
                store.update(suffixes(True))
            befores, passes, arrived, stride, done = carried(outflow, backward, beside)
            line, side = done[0]
            store.update(done[1])
        depth = len(befores)
        if final:
            wide = pair(2, block, 2 * LANES)
            body = partial(last_response_kernel, depth)
            out = call(body, wide + wide, (flags, *store["d"], *store["last"], *passes), 4 * unit)
            near, far = out[:2], out[2:]
            body = partial(base_kernel, depth)
            body = partial(lambda f, *refs: f(*refs[:-1], None, None, None, None, refs[-1]), body)
            (before,) = call(body, [trace], (*befores, *passes), unit)
            ins = (flags, line, side, *near, before)
            (base,) = call(last_base_kernel, [shape(2, block, columns)], ins, 2 * unit)
            body = partial(last_kernel, stride, backward)
            (x,) = call(body, [shape(2, block, columns)], (base, *far, arrived), 2 * unit)
            break
        if number == 0:
            store.update(suffixes(False))
        if ("join", backward) not in store:
            ins = (*store["side", backward], *passes)
            body = partial(join_kernel, depth)
            store["join", backward] = call(body, pair(3 * rows, 2 * LANES), ins, unit)
        base, before = call(
            partial(base_kernel, depth),
            [shape(2, rows, columns), trace],
            (*befores, *passes, side, *store["side", backward]),
            unit,
        )
        inflow, first, second = call(
            partial(enter_kernel, stride, backward, involution),
            [trace] * 3,
            (base, before, *store["join", backward], arrived),
            unit,
        )
        first, second = side_exchange(first, second, involution)
        base, start, left = call(
            partial(prepare_kernel, backward),
            [trace, field, field],
            (flags, inflow, line, store["z"], *store["d"], *store["e"], traces),
            14 * unit,
        )
    return x[None, None]


def solution(mesh):
    placed = (
        P("stream", "span", None, None, None),
        P("stream", "span", None, None, None),
        P(),
        P(),
        P(),
        P("stream", "span", None),
        P("stream", "span"),
        P("stream", "span", None, None),
        P("stream", "span", None, None),
    )
    return jax.shard_map(
        local,
        mesh=mesh,
        in_specs=placed,
        out_specs=P("stream", "span", None, None, None),
        check_vma=False,
    )
```
